32 devices in a mesh: wide: 8 (over z, core), rows: 4 (over y, x).
Axes of the slice: x: 2, y: 2, z: 4, core: 2. Of those that a mesh axis runs over, the one named last changes fastest.
Arguments:
- inputs: bfloat16 [8, 1024, 1024], P('rows', 'wide'), may hold values from -6 to 6
- lengths: int32 [8, 6], P('rows'), may hold values from 1 to 1019, as said below
- ffn1_in: bfloat16 [1024, 4096], P(('wide', 'rows')), may hold values from -0.1875 to 0.1875
- ffn1_out: bfloat16 [4096, 1024], P(('wide', 'rows')), may hold values from -0.1875 to 0.1875
- attn_qkv: bfloat16 [1024, 3072], P(('wide', 'rows')), may hold values from -0.1875 to 0.1875
- attn_out: bfloat16 [1024, 1024], P(('wide', 'rows')), may hold values from -0.75 to 0.75
- conv_in: bfloat16 [1024, 2048], P(('wide', 'rows')), may hold values from -0.1875 to 0.1875
- depth_kernel: bfloat16 [31, 1024], P(None, ('wide', 'rows')), may hold values from -1 to 1
- conv_out: bfloat16 [1024, 1024], P(('wide', 'rows')), may hold values from -0.375 to 0.375
- ffn2_in: bfloat16 [1024, 4096], P(('wide', 'rows')), may hold values from -0.1875 to 0.1875
- ffn2_out: bfloat16 [4096, 1024], P(('wide', 'rows')), may hold values from -0.1875 to 0.1875
- norm_gains: bfloat16 [6, 1024], P(None, ('wide', 'rows')), may hold values from 0.5 to 1.5
- cotangent: bfloat16 [8, 1024, 1024], P('rows', 'wide'), may hold values from -6 to 6
Outputs:
- layer_out: bfloat16 [8, 1024, 1024], P('rows', 'wide')
- grad_inputs: bfloat16 [8, 1024, 1024], P('rows', 'wide')
- grad_ffn1_in: float32 [1024, 4096], P(('wide', 'rows'))
- grad_ffn1_out: float32 [4096, 1024], P(('wide', 'rows'))
- grad_attn_qkv: float32 [1024, 3072], P(('wide', 'rows'))
- grad_attn_out: float32 [1024, 1024], P(('wide', 'rows'))
- grad_conv_in: float32 [1024, 2048], P(('wide', 'rows'))
- grad_depth_kernel: float32 [31, 1024], P(None, ('wide', 'rows'))
- grad_conv_out: float32 [1024, 1024], P(('wide', 'rows'))
- grad_ffn2_in: float32 [1024, 4096], P(('wide', 'rows'))
- grad_ffn2_out: float32 [4096, 1024], P(('wide', 'rows'))
- grad_norm_gains: float32 [6, 1024], P(None, ('wide', 'rows'))
The draws below stay inside these ranges and needn't reach their ends.
Inputs may be any that keep to these rules, and one draw needn't show every extreme that they name: The lengths of each row sum to 1024.
All inputs are finite; a program needn't handle non-finite values.
Results may differ from the reference program's by a relative error of at most 0.017.
Values may be sent and summed in bfloat16 or wider, within the bound.
No kernel may reach another device: no remote copies, remote signals or barrier semaphores. Data moves between devices by JAX's collectives and lax.ppermute only.
A program may use at most 256 MiB of HBM per device.

```python
import jax
import jax.numpy as jnp
from jax import lax

D = 1024
HEADS = 16
HEAD_DIM = 64
FF = 4096
KERNEL = 31
SEGS = 6
ROWS_DEV = 2
ROWS = 8
FRAMES = 1024


def draw_lengths(key, part):
    key = jax.random.fold_in(key, 11)
    key_pick = jax.random.fold_in(key, 0)
    key_long = jax.random.fold_in(key, 2)
    key_cut = jax.random.fold_in(key, 3)
    chosen = jax.random.randint(key_pick, (ROWS // ROWS_DEV,), 0, ROWS_DEV)
    row_index = jnp.arange(ROWS, dtype=jnp.int32)
    spanning = row_index % ROWS_DEV == jnp.repeat(chosen, ROWS_DEV)
    shorts = jnp.ones((ROWS, SEGS), jnp.int32)
    longest = jax.random.randint(key_long, (ROWS,), 0, SEGS)
    is_long = jnp.arange(SEGS, dtype=jnp.int32)[None, :] == longest[:, None]
    shorts = jnp.where(is_long, 0, shorts)
    span_lengths = jnp.where(is_long, FRAMES - jnp.sum(shorts, axis=1, keepdims=True, dtype=jnp.int32), shorts)
    cut_keys = jax.random.split(key_cut, ROWS)
    cuts = jax.vmap(lambda one_key: jnp.sort(jax.random.permutation(one_key, FRAMES - 1)[:SEGS - 1] + 1))(cut_keys)
    bounds = jnp.concatenate([jnp.zeros((ROWS, 1), jnp.int32), cuts.astype(jnp.int32), jnp.full((ROWS, 1), FRAMES, jnp.int32)], axis=1)
    ragged = bounds[:, 1:] - bounds[:, :-1]
    return jnp.where(spanning[:, None], span_lengths, ragged).astype(jnp.int32)


def steps_of(stream_key, shape, cuts, smallest, top_value):
    level, own = 1.0, jax.random.fold_in(stream_key, 6)
    for dim, blocks in cuts:
        steps = jnp.exp(jax.random.uniform(jax.random.fold_in(own, dim), (blocks,), jnp.float32, smallest / len(cuts), top_value / len(cuts)))
        level = level * jnp.repeat(steps, shape[dim] // blocks).reshape([-1 if axis == dim else 1 for axis in range(len(shape))])
    return level


def bell_draw(own_key, dims, scale, most, cuts=(), held_as=jnp.bfloat16):
    values = jax.random.normal(own_key, dims, jnp.float32) * scale
    if len(cuts) > 0:
        values = steps_of(own_key, dims, cuts, -0.22, 0.18) * values
    return jnp.clip(values, min=-most, max=most).astype(held_as)


def setup_inputs(seed: int = 0) -> dict:
    arg_keys = jax.random.split(jax.random.key(seed), 14)
    inputs = bell_draw(arg_keys[0], (ROWS, FRAMES, D), 1.0, 6.0, ((0, 4), (1, 8)))
    lengths = draw_lengths(jax.random.fold_in(arg_keys[13], 71), 0)
    ffn1_in = bell_draw(arg_keys[2], (D, FF), D ** -0.5, 0.1875, ((0, 32),))
    ffn1_out = bell_draw(arg_keys[3], (FF, D), (FF // 4) ** -0.5, 0.1875, ((0, 32),))
    attn_qkv = bell_draw(arg_keys[4], (D, 3 * D), D ** -0.5, 0.1875, ((0, 32),))
    attn_out = bell_draw(arg_keys[5], (D, D), (D // 16) ** -0.5, 0.75, ((0, 32),))
    conv_in = bell_draw(arg_keys[6], (D, 2 * D), D ** -0.5, 0.1875, ((0, 32),))
    depth_kernel = bell_draw(arg_keys[7], (KERNEL, D), KERNEL ** -0.5, 1.0, ((1, 32),))
    conv_out = bell_draw(arg_keys[8], (D, D), (D // 4) ** -0.5, 0.375, ((0, 32),))
    ffn2_in = bell_draw(arg_keys[9], (D, FF), D ** -0.5, 0.1875, ((0, 32),))
    ffn2_out = bell_draw(arg_keys[10], (FF, D), (FF // 4) ** -0.5, 0.1875, ((0, 32),))
    norm_gains = jnp.clip(1.0 + 0.1 * jax.random.normal(arg_keys[11], (6, D), jnp.float32), 0.5, 1.5).astype(jnp.bfloat16)
    cotangent = bell_draw(arg_keys[12], (ROWS, FRAMES, D), 1.0, 6.0, ((0, 4), (1, 8)))
    return {"inputs": inputs, "lengths": lengths, "ffn1_in": ffn1_in, "ffn1_out": ffn1_out, "attn_qkv": attn_qkv, "attn_out": attn_out, "conv_in": conv_in, "depth_kernel": depth_kernel, "conv_out": conv_out, "ffn2_in": ffn2_in, "ffn2_out": ffn2_out, "norm_gains": norm_gains, "cotangent": cotangent}


EPSILON = 1e-05
HIGHEST = lax.Precision.HIGHEST

@jax.custom_vjp
def low(v):
    return lax.optimization_barrier(v.astype(jnp.bfloat16)).astype(jnp.float32)

@jax.custom_vjp
def low_back(v):
    return v

def low_keep(v):
    return (low(v), None)

def low_pass(kept, grad):
    return (grad,)

def back_keep(v):
    return (v, None)

def back_low(kept, grad):
    return (low(grad),)
low.defvjp(low_keep, low_pass)
low_back.defvjp(back_keep, back_low)

def segment_info(lengths, frame_total):
    segment_end = jnp.cumsum(lengths, axis=-1, dtype=jnp.int32)
    frame_index = jnp.arange(frame_total, dtype=jnp.int32)
    passed = (frame_index[None, None, :] >= segment_end[:, :, None]).astype(jnp.int32)
    segment_ids = lax.optimization_barrier(jnp.sum(passed, axis=1, dtype=jnp.int32))
    seg_starts = lax.optimization_barrier(jnp.sum(passed * lengths[:, :, None], axis=1, dtype=jnp.int32))
    return (segment_ids, frame_index[None, :] - seg_starts)

def layer_norm(values, gain_row):
    centred = values - lax.optimization_barrier(jnp.mean(values, axis=-1, keepdims=True))
    variance = lax.optimization_barrier(jnp.mean(centred * centred, axis=-1, keepdims=True))
    return centred * lax.rsqrt(variance + EPSILON) * gain_row

def project(left, right):
    return jnp.einsum('rfd,de->rfe', left, right, precision=HIGHEST)

def rotation(position, head_size):
    half_width = head_size // 2
    frequency = jnp.power(10000.0, -2.0 * jnp.arange(half_width, dtype=jnp.float32) / head_size)
    angles = position.astype(jnp.float32)[..., None] * frequency
    return (jnp.cos(angles)[..., None, :], jnp.sin(angles)[..., None, :])

def rotate(values, cosine, sine):
    half_width = values.shape[-1] // 2
    front_half = values[..., :half_width]
    back_half = values[..., half_width:]
    return jnp.concatenate([front_half * cosine - back_half * sine, front_half * sine + back_half * cosine], axis=-1)

def attend(items):
    queries, keys, values, segment_ids = items
    scale_factor = queries.shape[-1] ** (-0.5)
    scores = low_back(jnp.einsum('qhd,khd->hqk', queries, keys, precision=HIGHEST) * scale_factor)
    same_segment = segment_ids[:, None] == segment_ids[None, :]
    scores = jnp.where(same_segment[None], scores, -1e+30)
    row_max = lax.optimization_barrier(jnp.max(scores, axis=-1, keepdims=True))
    unnormed = jnp.exp(scores - row_max)
    probabilities = low(unnormed / lax.optimization_barrier(jnp.sum(unnormed, axis=-1, keepdims=True)))
    return jnp.einsum('hqk,khd->qhd', probabilities, values, precision=HIGHEST)

def feed_forward(residual, gain_row, weight_in, weight_out):
    hidden = low(layer_norm(residual, gain_row))
    before = low_back(project(hidden, weight_in))
    after = low(before * jax.nn.sigmoid(before))
    return residual + 0.5 * low_back(project(after, weight_out))

def reference(inputs, lengths, ffn1_in, ffn1_out, attn_qkv, attn_out, conv_in, depth_kernel, conv_out, ffn2_in, ffn2_out, norm_gains, cotangent):
    segment_ids, position = segment_info(lengths, FRAMES)
    cosine, sine = rotation(position, HEAD_DIM)
    half_width = KERNEL // 2
    padded_ids = jnp.pad(segment_ids, ((0, 0), (half_width, half_width)), constant_values=-1)
    tap_masks = [(padded_ids[:, tap_index:tap_index + FRAMES] == segment_ids).astype(jnp.float32)[..., None] for tap_index in range(KERNEL)]
    heads_shape = (ROWS, FRAMES, HEADS, HEAD_DIM)

    def forward(residual, params):
        gains = params[9]
        first = feed_forward(residual, gains[0], params[0], params[1])
        hidden = low(layer_norm(first, gains[1]))
        packed = low_back(project(hidden, params[2]))
        queries = low(rotate(packed[..., :D].reshape(heads_shape), cosine, sine))
        keys = low(rotate(packed[..., D:2 * D].reshape(heads_shape), cosine, sine))
        values = low(packed[..., 2 * D:].reshape(heads_shape))
        mixed = lax.map(jax.checkpoint(attend), (queries, keys, values, segment_ids))
        mixed = low(low_back(mixed.reshape(ROWS, FRAMES, D)))
        second = first + low_back(project(mixed, params[3]))
        hidden = low(layer_norm(second, gains[2]))
        gated = low_back(project(hidden, params[4]))
        glu = low(gated[..., :D] * jax.nn.sigmoid(gated[..., D:]))
        padded = jnp.pad(glu, ((0, 0), (half_width, half_width), (0, 0)))
        convolved = jnp.zeros_like(glu)
        for tap_index in range(KERNEL):
            convolved = convolved + padded[:, tap_index:tap_index + FRAMES] * params[5][tap_index] * tap_masks[tap_index]
        normed = layer_norm(convolved, gains[3])
        activated = low(normed * jax.nn.sigmoid(normed))
        third = second + low_back(project(activated, params[6]))
        fourth = feed_forward(third, gains[4], params[7], params[8])
        return layer_norm(fourth, gains[5])
    params = tuple((weight.astype(jnp.float32) for weight in (ffn1_in, ffn1_out, attn_qkv, attn_out, conv_in, depth_kernel, conv_out, ffn2_in, ffn2_out, norm_gains)))
    result, pullback = jax.vjp(forward, inputs.astype(jnp.float32), params)
    grad_input, grad_params = pullback(cotangent.astype(jnp.float32))
    return (result.astype(jnp.bfloat16), grad_input.astype(jnp.bfloat16), grad_params[0], grad_params[1], grad_params[2], grad_params[3], grad_params[4], grad_params[5], grad_params[6], grad_params[7], grad_params[8], grad_params[9])
```

```python
import functools

import jax
import jax.numpy as jnp
import numpy as np
from jax import lax
from jax.experimental import pallas as pl
from jax.experimental.pallas import tpu as pltpu
from jax.sharding import PartitionSpec as P

HEADS = 16
HEAD_DIM = 64
EPSILON = 1e-05
BOTH = ("wide", "rows")
F32 = jnp.float32
BF16 = jnp.bfloat16
HIGHEST = lax.Precision.HIGHEST
VMEM_LIMIT = 60 * 1024 * 1024


class Plan:
    def __init__(self, wide, rows):
        self.wide, self.rows, self.total = wide, rows, wide * rows
        self.far = [k * 2 * rows for k in range(1, wide // 2)]
        row_bits = [1 << b for b in range(rows.bit_length() - 1)]
        self.flips = (row_bits, row_bits[1:] + row_bits[:1])
        self.stages = len(row_bits)
        self.far_bits = [1 << b for b in range((wide // 2).bit_length() - 1)]
        self.blocks = self.total // 2
        self.table = [
            np.array(
                [
                    far ^ sum(f for t, f in enumerate(flips) if p >> t & 1)
                    for p in range(1 << self.stages)
                    for far in [0, *self.far]
                ],
                np.int32,
            )
            for flips in self.flips
        ]

    def core_of(self, index):
        return (index // self.rows) % 2

    def stage_pairs(self, stage):
        return [(i, i ^ self.flips[self.core_of(i)][stage]) for i in range(self.total)]

    def flip_pairs(self, flip):
        return [(i, i ^ flip) for i in range(self.total)]

    def orders(self):
        index = lax.axis_index(BOTH)
        core = self.core_of(index)
        table = jnp.stack([jnp.asarray(t) for t in self.table])
        own = index ^ jnp.take(table, core, axis=0)
        other = (index ^ self.rows) ^ jnp.take(table, 1 - core, axis=0)
        return own, other


def send(x, pairs):
    return lax.ppermute(x, BOTH, pairs)


def held(arrays):
    return [pl.BlockSpec(memory_space=pl.ANY)] * len(arrays)


def there(tokens, before=None):
    tokens = jax.tree.leaves((tokens, before))
    if not tokens:
        return None

    def kernel(*refs):
        refs[-1][0] = 1

    return pl.pallas_call(
        kernel,
        out_shape=jax.ShapeDtypeStruct((1,), jnp.int32),
        in_specs=held(tokens),
        out_specs=pl.BlockSpec(memory_space=pltpu.SMEM),
        cost_estimate=pl.CostEstimate(flops=0, transcendentals=0, bytes_accessed=0),
        name="there",
    )(*tokens)


def after(values, tokens, before=None):
    flag = there(tokens, before) if jax.tree.leaves(tokens) else before
    if flag is None or not jax.tree.leaves(values):
        return values
    flag = flag[0] > 0
    return jax.tree.map(lambda x: jnp.where(flag, x, jnp.zeros((), x.dtype)), values)


class Lane:
    def __init__(self, steps):
        self.steps, self.result, self.arriving = steps, None, None
        self.operand, self.pairs = next(steps)

    def go(self):
        if isinstance(self.pairs[0], list):
            self.arriving = [send(x, pairs) for x, pairs in zip(self.operand, self.pairs)]
        else:
            self.arriving = jax.tree.map(lambda x: send(x, self.pairs), self.operand)

    def landed(self, arrived):
        self.arriving = None
        try:
            self.operand, self.pairs = self.steps.send(arrived)
        except StopIteration as stop:
            self.operand, self.result = None, stop.value


def step(land=(), go=(), chain=(), since=()):
    land = [lane for lane in land if lane.arriving is not None]
    flag = there(list(since)) if since else None
    for lane in land:
        lane.landed(after(lane.arriving, [], flag))
    if jax.tree.leaves(chain):
        chain = after(chain, jax.tree.leaves(ready(*land)))
    for lane in go:
        if lane.operand is not None and lane.arriving is None:
            lane.go()
    return chain


def hold(lane, *tokens):
    lane.operand = after(lane.operand, list(tokens))
    lane.go()


def waited(*lanes):
    return [lane.arriving for lane in lanes if lane.arriving is not None]


def ready(*lanes):
    return [lane.operand for lane in lanes if lane.operand is not None]


def finish(*lanes):
    while any(lane.operand is not None for lane in lanes):
        for lane in lanes:
            step(land=[lane], go=[lane])
    return lanes[0].result


def gather_lane(plan, shard, finish):
    held = shard[None]
    for bit in reversed(plan.far_bits):
        pairs = plan.flip_pairs(bit * 2 * plan.rows)
        arrived = yield held, pairs
        held = jnp.stack([held, arrived], axis=1).reshape(-1, *shard.shape)
    for stage in range(plan.stages - 1):
        held = jnp.concatenate([held, (yield held, plan.stage_pairs(stage))], axis=0)
    last = yield held, plan.stage_pairs(plan.stages - 1)
    from_core = yield [held, last], plan.flip_pairs(plan.rows)
    return finish([held, last, *from_core])


def grad_lane(plan, own, other, right, small=None):
    swapped = yield [other, right], plan.flip_pairs(plan.rows)
    left = jnp.concatenate([own, swapped[0]], axis=0)
    both = jnp.concatenate([right, swapped[1]], axis=0)
    left, both = lax.optimization_barrier((left, both))
    half = left.shape[1] // 2
    away = [dot_over_frames(left[:, half:], both).astype(BF16)]
    kept = None
    if small:
        little = small()
        columns = little.shape[1] // 2
        away.append(after(little[:, columns:], away[0]))
        little = little[:, :columns]
    for stage in reversed(range(plan.stages)):
        arrived = yield away, plan.stage_pairs(stage)
        if kept is None:
            kept = dot_over_frames(left[:, :half], both).astype(BF16)
        if small:
            little = little + after(arrived[1], arrived[0])
        if stage > 0:
            half = kept.shape[0] // 2
            away = [(kept[half:].astype(F32) + arrived[0][half:].astype(F32)).astype(BF16)]
            kept = kept[:half].astype(F32) + arrived[0][:half].astype(F32)
            kept = kept.astype(BF16)
            if small:
                columns = little.shape[1] // 2
                away.append(little[:, columns:])
                little = little[:, :columns]
    size = kept.shape[0] // (len(plan.far) + 1)
    away = []
    for block in range(1, len(plan.far) + 1):
        rows = slice(block * size, (block + 1) * size)
        away.append([(kept[rows].astype(F32) + arrived[0][rows].astype(F32)).astype(BF16)])
    total = kept[:size].astype(F32) + arrived[0][:size].astype(F32)
    if small:
        size = little.shape[1] // (len(plan.far) + 1)
        for block in range(1, len(plan.far) + 1):
            away[block - 1].append(little[:, block * size : (block + 1) * size])
        little = little[:, :size]
    arrived = yield (
        [x for pair in away for x in pair],
        [plan.flip_pairs(far) for far in plan.far for _ in range(2 if small else 1)],
    )
    step = 2 if small else 1
    for one in arrived[::step]:
        total = total + one.astype(F32)
    if small:
        little = little + sum(after(arrived[1::2], arrived[::2]))
    return (total, little) if small else total


def heads_lane(plan, x):
    sent = x.reshape(plan.wide // 2, 2, *x.shape[1:])
    from_core = yield sent[:, 1], plan.flip_pairs(plan.rows)
    pair = jnp.stack([sent[:, 0], from_core], axis=1)
    arrived = yield (
        [pair[k] for k in range(1, plan.wide // 2)],
        [plan.flip_pairs(far) for far in plan.far],
    )
    return jnp.stack([pair[0], *arrived]).reshape(x.shape)


def assemble(plan, pieces, shapes, orders):
    half = plan.blocks // 2
    width = pieces[0].shape[-1]
    index = jnp.concatenate(orders)
    if any(rows % 16 for rows, _ in shapes):
        stacked = jnp.concatenate(pieces, axis=0)
        place = jnp.zeros((plan.total,), jnp.int32).at[index].set(jnp.arange(plan.total))
        stacked = jnp.take(stacked, place, axis=0)
        outs, start = [], 0
        for rows, columns in shapes:
            parts = []
            for _ in range(columns // width):
                parts.append(stacked[:, start : start + rows].reshape(-1, width))
                start += rows
            outs.append(jnp.concatenate(parts, axis=1))
        return outs

    def kernel(order, *refs):
        sources, outs = refs[:4], refs[4:-3]
        held, in_sems, out_sems = refs[-3:]
        loads = [
            pltpu.make_async_copy(sources[which], held.at[which], in_sems.at[which])
            for which in range(4)
        ]
        for load in loads:
            load.start()
        for which in range(4):
            loads[which].wait()
            for place in range(half):
                block = order[which * half + place]
                start = 0
                for out, (rows, columns) in enumerate(shapes):
                    for part in range(columns // width):
                        pltpu.make_async_copy(
                            held.at[which, place, pl.ds(start, rows)],
                            outs[out].at[
                                pl.ds(pl.multiple_of(block * rows, rows), rows),
                                pl.ds(part * width, width),
                            ],
                            out_sems.at[out],
                        ).start()
                        start += rows
        for out in range(len(shapes)):
            pltpu.make_async_copy(outs[out], outs[out], out_sems.at[out]).wait()

    return pl.pallas_call(
        kernel,
        out_shape=[
            jax.ShapeDtypeStruct((rows * plan.total, columns), BF16) for rows, columns in shapes
        ],
        in_specs=[pl.BlockSpec(memory_space=pltpu.SMEM)] + [pl.BlockSpec(memory_space=pl.ANY)] * 4,
        out_specs=[pl.BlockSpec(memory_space=pl.ANY)] * len(shapes),
        scratch_shapes=[
            pltpu.VMEM((4,) + pieces[0].shape, BF16),
            pltpu.SemaphoreType.DMA((4,)),
            pltpu.SemaphoreType.DMA((len(shapes),)),
        ],
        compiler_params=pltpu.CompilerParams(vmem_limit_bytes=24 * 1024 * 1024),
        cost_estimate=pl.CostEstimate(
            flops=0, transcendentals=0, bytes_accessed=8 * pieces[0].size * 2
        ),
        name="assemble",
    )(index, *pieces)


def pick_columns(plan, x, orders):
    index = jnp.concatenate(orders)
    length, columns = x.shape
    size = columns // plan.total
    if size % 128:
        split = jnp.take(x.reshape(length, plan.total, size), index, axis=1)
        split = split.reshape(length, columns)
        return split[:, : columns // 2], split[:, columns // 2 :]

    def kernel(order, source, first, second):
        for place in range(plan.total):
            out = (first, second)[place // plan.blocks]
            start = pl.multiple_of(order[place] * size, size)
            out[:, pl.ds((place % plan.blocks) * size, size)] = source[:, pl.ds(start, size)]

    whole = pl.BlockSpec(memory_space=pltpu.VMEM)
    return pl.pallas_call(
        kernel,
        out_shape=[jax.ShapeDtypeStruct((length, columns // 2), x.dtype)] * 2,
        in_specs=[pl.BlockSpec(memory_space=pltpu.SMEM), whole],
        out_specs=[whole] * 2,
        compiler_params=pltpu.CompilerParams(vmem_limit_bytes=16 * 1024 * 1024),
        cost_estimate=pl.CostEstimate(
            flops=0, transcendentals=0, bytes_accessed=4 * x.size
        ),
        name="pick_columns",
    )(index, x)


def dot(left, right):
    return jnp.dot(left, right, preferred_element_type=F32)


def dot_back(left, right):
    return lax.dot_general(left, right, (((1,), (1,)), ((), ())), preferred_element_type=F32)


def dot_over_frames(left, right):
    return lax.dot_general(left, right, (((0,), (0,)), ((), ())), preferred_element_type=F32)


def head_lanes(size, head):
    lane = lax.broadcasted_iota(jnp.int32, (1, size), 1)
    return (lane >= head * HEAD_DIM) & (lane < (head + 1) * HEAD_DIM)


def attend_kernel(q_ref, k_ref, v_ref, idq_ref, idk_ref, o_ref, total_ref):
    size = q_ref.shape[-1]
    query, keys, values = q_ref[0] * HEAD_DIM**-0.5, k_ref[0], v_ref[0]
    same = idq_ref[0] == idk_ref[0]
    mixed = jnp.zeros(query.shape, F32)
    totals = []
    for head in range(size // HEAD_DIM):
        lanes = head_lanes(size, head)
        scores = lax.dot_general(
            jnp.where(lanes, query, 0), keys, (((1,), (1,)), ((), ())), preferred_element_type=F32
        )
        scores = jnp.where(same, scores, -1e30)
        most = jnp.max(scores, axis=-1, keepdims=True)
        unnormed = jnp.exp(scores - most)
        total = jnp.sum(unnormed, axis=-1, keepdims=True)
        probs = (unnormed * (1.0 / total)).astype(BF16)
        mixed += jnp.dot(probs, jnp.where(lanes, values, 0), preferred_element_type=F32)
        totals.append(most + jnp.log(total))
    o_ref[0] = mixed.astype(BF16)
    total_ref[0] = jnp.concatenate(totals, axis=1)


def attend_back_kernel(
    q_ref, k_ref, v_ref, o_ref, do_ref, total_ref, idq_ref, idk_ref, cq_ref, sq_ref, ck_ref,
    sk_ref, turn_ref, dq_ref, dk_ref, dv_ref, dk_sum, dv_sum,
):
    step = pl.program_id(1)
    size = q_ref.shape[-1]
    scale = HEAD_DIM**-0.5
    query, keys, values, grads = q_ref[0] * scale, k_ref[0], v_ref[0], do_ref[0]
    different = idk_ref[0] != idq_ref[0]
    product = grads.astype(F32) * o_ref[0].astype(F32)

    @pl.when(step == 0)
    def _():
        dk_sum[...] = jnp.zeros_like(dk_sum)
        dv_sum[...] = jnp.zeros_like(dv_sum)

    turned_sum = jnp.zeros((size, query.shape[0]), F32)
    for head in range(size // HEAD_DIM):
        lanes = head_lanes(size, head)
        one_query = jnp.where(lanes, query, 0)
        one_grad = jnp.where(lanes, grads, 0)
        delta = lax.dot_general(
            jnp.where(lanes, jnp.ones((8, size), F32), 0.0),
            product,
            (((1,), (1,)), ((), ())),
            precision=HIGHEST,
            preferred_element_type=F32,
        )[:1]
        scores = lax.dot_general(
            keys, one_query, (((1,), (1,)), ((), ())), preferred_element_type=F32
        )
        probs = jnp.exp(jnp.where(different, -1e30, scores - total_ref[0, head : head + 1]))
        prob_grads = lax.dot_general(
            values, one_grad, (((1,), (1,)), ((), ())), preferred_element_type=F32
        )
        score_grads = (probs * (prob_grads - delta)).astype(BF16)
        dk_sum[...] += jnp.dot(score_grads, one_query, preferred_element_type=F32)
        dv_sum[...] += jnp.dot(probs.astype(BF16), one_grad, preferred_element_type=F32)
        turned_sum += dot_over_frames(jnp.where(lanes, keys, 0), score_grads)

    def turned(grad, cosine, sine):
        partner = jnp.dot(grad, turn_ref[...], precision=HIGHEST, preferred_element_type=F32)
        return (grad * cosine + partner * sine).astype(BF16)

    dq_ref[0] = turned(turned_sum.T * scale, cq_ref[0], sq_ref[0])

    @pl.when(step == pl.num_programs(1) - 1)
    def _():
        dk_ref[0] = turned(dk_sum[...], ck_ref[0], sk_ref[0])
        dv_ref[0] = dv_sum[...].astype(BF16)


def attend(query, keys, values, ids, tokens=()):
    rows, length, size = query.shape
    tile = 256
    heads = size // HEAD_DIM
    whole = pl.BlockSpec((1, length, size), lambda r, t: (r, 0, 0))
    part = pl.BlockSpec((1, tile, size), lambda r, t: (r, t, 0))
    return pl.pallas_call(
        lambda *refs: attend_kernel(*refs[:5], *refs[5 + len(tokens) :]),
        out_shape=[
            jax.ShapeDtypeStruct(query.shape, BF16),
            jax.ShapeDtypeStruct((rows, length, heads), F32),
        ],
        grid=(rows, length // tile),
        in_specs=[
            part,
            whole,
            whole,
            pl.BlockSpec((1, tile, 1), lambda r, t: (r, t, 0)),
            pl.BlockSpec((1, 1, length), lambda r, t: (r, 0, 0)),
            *held(tokens),
        ],
        out_specs=[part, pl.BlockSpec((1, tile, heads), lambda r, t: (r, t, 0))],
        compiler_params=pltpu.CompilerParams(vmem_limit_bytes=VMEM_LIMIT),
        name="attend",
    )(query, keys, values, ids[:, :, None], ids[:, None, :], *tokens)


def attend_back(query, keys, values, mixed, grads, totals, ids, cosine, sine, tokens=()):
    rows, length, size = query.shape
    tile = 256
    heads = size // HEAD_DIM
    whole = pl.BlockSpec((1, length, size), lambda r, t: (r, 0, 0))
    part = pl.BlockSpec((1, tile, size), lambda r, t: (r, t, 0))
    lane = np.arange(size)
    turn = jnp.asarray((lane[:, None] == (lane ^ (HEAD_DIM // 2))[None, :]).astype(np.float32))
    return pl.pallas_call(
        lambda *refs: attend_back_kernel(*refs[:13], *refs[13 + len(tokens) :]),
        out_shape=[jax.ShapeDtypeStruct(query.shape, BF16)] * 3,
        grid=(rows, length // tile),
        in_specs=[
            part,
            whole,
            whole,
            part,
            part,
            pl.BlockSpec((1, heads, tile), lambda r, t: (r, 0, t)),
            pl.BlockSpec((1, 1, tile), lambda r, t: (r, 0, t)),
            pl.BlockSpec((1, length, 1), lambda r, t: (r, 0, 0)),
            part,
            part,
            whole,
            whole,
            pl.BlockSpec((size, size), lambda r, t: (0, 0)),
            *held(tokens),
        ],
        out_specs=[part, whole, whole],
        scratch_shapes=[pltpu.VMEM((length, size), F32)] * 2,
        compiler_params=pltpu.CompilerParams(vmem_limit_bytes=VMEM_LIMIT),
        name="attend_back",
    )(
        query, keys, values, mixed, grads, totals.transpose(0, 2, 1), ids[:, None, :],
        ids[:, :, None], cosine, sine, cosine, sine, turn, *tokens,
    )


def set_masks(ids_ref, ids, masks, count):
    ids[...] = jnp.broadcast_to(ids_ref[0], ids.shape)
    here = ids[pl.ds(masks.shape[0] // 2, count)]
    for tap in range(masks.shape[0]):
        masks[tap] = jnp.where(ids[pl.ds(tap, count)] == here, 1.0, 0.0)


def conv_kernel(ext_ref, ids_ref, taps_ref, out_ref, frames, ids, masks):
    count, taps = out_ref.shape[1], taps_ref.shape[0]

    @pl.when(pl.program_id(1) == 0)
    def _():
        set_masks(ids_ref, ids, masks, count)

    frames[...] = ext_ref[0].astype(F32)
    total = jnp.zeros((count, frames.shape[1]), F32)
    for odd in range(8):
        shifted = frames[pl.ds(odd, frames.shape[0] - 8)]
        for tap in range(odd, taps, 8):
            part = shifted[tap - odd : tap - odd + count]
            total += part * masks[tap] * taps_ref[tap : tap + 1]
    out_ref[0] = total


def conv_back_kernel(
    ext_ref, ids_ref, grad_ref, taps_ref, dtaps_ref, dext_ref, frames, ids, masks, total, some
):
    count, taps = grad_ref.shape[1], taps_ref.shape[0]

    @pl.when(pl.program_id(1) == 0)
    def _():
        set_masks(ids_ref, ids, masks, count)

    frames[...] = ext_ref[0].astype(F32)
    grad = grad_ref[0]
    total[...] = jnp.zeros_like(total)
    rows = [None] * taps
    for odd in range(8):
        shifted = frames[pl.ds(odd, frames.shape[0] - 8)]
        some[...] = jnp.zeros_like(some)
        for tap in range(odd, taps, 8):
            kept = grad * masks[tap]
            rows[tap] = jnp.sum(shifted[tap - odd : tap - odd + count] * kept, axis=0, keepdims=True)
            some[pl.ds(tap - odd, count)] += kept * taps_ref[tap : tap + 1]
        total[pl.ds(odd, some.shape[0])] += some[...]
    dext_ref[0] = total[...]
    dtaps_ref[0] = jnp.concatenate(rows, axis=0)


def depthwise(extended, ids, taps, tokens=()):
    rows, padded, width = extended.shape
    count = padded - 32
    block = 128
    return pl.pallas_call(
        lambda *refs: conv_kernel(*refs[:3], *refs[3 + len(tokens) :]),
        out_shape=jax.ShapeDtypeStruct((rows, count, width), F32),
        grid=(rows, width // block),
        in_specs=[
            pl.BlockSpec((1, padded, block), lambda r, c: (r, 0, c)),
            pl.BlockSpec((1, padded, 1), lambda r, c: (r, 0, 0)),
            pl.BlockSpec((taps.shape[0], block), lambda r, c: (0, c)),
            *held(tokens),
        ],
        out_specs=pl.BlockSpec((1, count, block), lambda r, c: (r, 0, c)),
        scratch_shapes=[pltpu.VMEM((padded, block), F32)] * 2
        + [pltpu.VMEM((taps.shape[0], count, block), F32)],
        compiler_params=pltpu.CompilerParams(vmem_limit_bytes=16 * 1024 * 1024),
        name="depthwise",
    )(extended, ids, taps, *tokens)


def depthwise_back(extended, ids, grad, taps, tokens=()):
    rows, padded, width = extended.shape
    count = padded - 32
    block = 128
    return pl.pallas_call(
        lambda *refs: conv_back_kernel(*refs[:4], *refs[4 + len(tokens) :]),
        out_shape=[
            jax.ShapeDtypeStruct((rows, taps.shape[0], width), F32),
            jax.ShapeDtypeStruct((rows, padded, width), F32),
        ],
        grid=(rows, width // block),
        in_specs=[
            pl.BlockSpec((1, padded, block), lambda r, c: (r, 0, c)),
            pl.BlockSpec((1, padded, 1), lambda r, c: (r, 0, 0)),
            pl.BlockSpec((1, count, block), lambda r, c: (r, 0, c)),
            pl.BlockSpec((taps.shape[0], block), lambda r, c: (0, c)),
            *held(tokens),
        ],
        out_specs=[
            pl.BlockSpec((1, taps.shape[0], block), lambda r, c: (r, 0, c)),
            pl.BlockSpec((1, padded, block), lambda r, c: (r, 0, c)),
        ],
        scratch_shapes=[pltpu.VMEM((padded, block), F32)] * 2
        + [
            pltpu.VMEM((taps.shape[0], count, block), F32),
            pltpu.VMEM((padded, block), F32),
            pltpu.VMEM((padded - 8, block), F32),
        ],
        compiler_params=pltpu.CompilerParams(vmem_limit_bytes=16 * 1024 * 1024),
        name="depthwise_back",
    )(extended, ids, grad, taps, *tokens)


def segment_info(lengths, frame_total):
    segment_end = jnp.cumsum(lengths, axis=-1, dtype=jnp.int32)
    frame_index = jnp.arange(frame_total, dtype=jnp.int32)
    passed = (frame_index[None, None, :] >= segment_end[:, :, None]).astype(jnp.int32)
    segment_ids = jnp.sum(passed, axis=1, dtype=jnp.int32)
    seg_starts = jnp.sum(passed * lengths[:, :, None], axis=1, dtype=jnp.int32)
    return (segment_ids, frame_index[None, :] - seg_starts)


def layer_norm(values, gain_row):
    centred = values - jnp.mean(values, axis=-1, keepdims=True)
    inv_scale = lax.rsqrt(jnp.mean(centred * centred, axis=-1, keepdims=True) + EPSILON)
    normed = centred * inv_scale
    return (normed * gain_row, normed, inv_scale)


def norm_backward(gradient, gain_row, normed, inv_scale):
    scaled = gradient * gain_row
    gain_grad = jnp.sum(gradient * normed, axis=0)
    centred_mean = jnp.mean(scaled, axis=-1, keepdims=True)
    product_mean = jnp.mean(scaled * normed, axis=-1, keepdims=True)
    return (inv_scale * (scaled - centred_mean - normed * product_mean), gain_grad)


def swish_slope(values):
    gate_sig = jax.nn.sigmoid(values)
    return gate_sig * (1.0 + values * (1.0 - gate_sig))


def neighbours(x, width, axis):
    size, length = lax.axis_size("wide"), x.shape[axis]
    up = [(i, i + 1) for i in range(size - 1)]
    before = lax.ppermute(lax.slice_in_dim(x, length - width, length, axis=axis), "wide", up)
    after = lax.ppermute(
        lax.slice_in_dim(x, 0, width, axis=axis), "wide", [(j, i) for i, j in up]
    )
    return before, after


def half_turn(values):
    half = HEAD_DIM // 2
    lane = lax.broadcasted_iota(jnp.int32, (1, values.shape[-1]), 1) % HEAD_DIM
    ahead = jnp.roll(values, -half, axis=-1)
    behind = jnp.roll(values, half, axis=-1)
    return jnp.where(lane < half, -ahead, behind)


def per_device(
    inputs,
    lengths,
    ffn1_in,
    ffn1_out,
    attn_qkv,
    attn_out,
    conv_in,
    depth_kernel,
    conv_out,
    ffn2_in,
    ffn2_out,
    norm_gains,
    cotangent,
):
    wide, rows = lax.axis_size("wide"), lax.axis_size("rows")
    plan = Plan(wide, rows)
    row_count, frames_here, width = inputs.shape
    tokens = row_count * frames_here
    frame_total = frames_here * wide
    taps = depth_kernel.shape[0]
    half_width = taps // 2
    me = lax.axis_index("wide")
    orders = plan.orders()
    segment_ids, position = segment_info(lengths, frame_total)

    def packed_shards(shards):
        parts = []
        for shard in shards:
            for column in range(0, shard.shape[1], width):
                parts.append(shard[:, column : column + width])
        return jnp.concatenate(parts, axis=0) if len(parts) > 1 else parts[0]

    def weights_lane(*shards):
        shapes = [shard.shape for shard in shards]
        return Lane(
            gather_lane(
                plan, packed_shards(shards), lambda held: assemble(plan, held, shapes, orders)
            )
        )

    def small_lane(small):
        flip = 1
        while flip < plan.total:
            small = jnp.concatenate([small, (yield small, plan.flip_pairs(flip))], axis=1)
            flip *= 2
        return dot_back(small, small_pick.astype(BF16))

    feature = jnp.arange(width, dtype=jnp.int32)
    block = width // plan.total
    small_source = (feature // block ^ lax.axis_index(BOTH)) * block + feature % block
    small_pick = feature[:, None] == small_source[None, :]
    small = Lane(small_lane(jnp.concatenate([norm_gains, depth_kernel], axis=0)))
    g1, g2 = weights_lane(ffn1_in), weights_lane(ffn1_out)
    w_qkv = lax.all_gather(attn_qkv, BOTH, axis=0, tiled=True)
    wides = (attn_out, conv_in, conv_out, ffn2_in)

    def late_weights(*tokens):
        shards = after((jnp.concatenate(wides, axis=1), ffn2_out), list(tokens))
        middle = lax.all_gather(shards[0], BOTH, axis=0, tiled=True)
        cuts = np.cumsum([0] + [shard.shape[1] for shard in wides])
        parts = tuple(middle[:, start:stop] for start, stop in zip(cuts[:-1], cuts[1:]))
        return parts + (lax.all_gather(shards[1], BOTH, axis=0, tiled=True),)

    source = jnp.repeat(jnp.concatenate(orders), block) * block + feature % block
    tree_pick = (feature[:, None] == source[None, :]).astype(BF16)
    group = width // wide
    head_source = (feature // group ^ me) * group + feature % group
    head_pick = (feature[:, None] == head_source[None, :]).astype(BF16)

    def pick(x):
        both = dot(x, tree_pick).astype(BF16)
        return both[:, : width // 2], both[:, width // 2 :]

    def to_groups(x):
        return dot(x, head_pick).astype(BF16).reshape(tokens, wide, group).transpose(1, 0, 2)

    def from_groups(x):
        return dot_back(x.transpose(1, 0, 2).reshape(tokens, width), head_pick).astype(BF16)

    offset = me * frames_here
    padded_ids = jnp.pad(segment_ids, ((0, 0), (half_width, 32 - half_width)), constant_values=-1)
    edge_ids = lax.dynamic_slice_in_dim(padded_ids, offset, frames_here + 32, 1)
    edge_ids = edge_ids.astype(F32)[:, :, None]
    local_position = lax.dynamic_slice_in_dim(position, offset, frames_here, 1)
    by_device = jnp.arange(wide, dtype=jnp.int32) ^ me

    def row_order(x):
        x = x.reshape(row_count, wide, frames_here)
        return jnp.take(x, by_device, axis=1).reshape(row_count, frame_total)

    row_ids, row_position = row_order(segment_ids), row_order(position)

    def rotation(at, size):
        lane = jnp.arange(size, dtype=jnp.int32) % HEAD_DIM
        frequency = jnp.power(
            10000.0, -2.0 * (lane % (HEAD_DIM // 2)).astype(F32) / HEAD_DIM
        )
        angles = at.astype(F32)[..., None] * frequency
        sign = jnp.where(lane < HEAD_DIM // 2, 1.0, -1.0)
        return jnp.cos(angles), jnp.sin(angles), sign

    cosine, sine, _ = rotation(local_position.reshape(tokens), HEAD_DIM)
    cosine = jnp.tile(cosine, (1, HEADS))
    sine = jnp.tile(sine, (1, HEADS))
    row_cosine, row_sine, sign = rotation(row_position, group)
    row_sine = row_sine * sign

    tables = (row_cosine, row_sine, cosine, sine, edge_ids)
    def follow(lane, leader):
        lane.operand = after(lane.operand, jax.tree.leaves(ready(leader)))
        lane.go()

    step(go=[g1, small])
    for _ in range(3):
        step(land=[small], go=[small])
    step(land=[g1, small], go=[small])
    follow(g1, small)
    finish(small)
    gains, kernel = small.result[: norm_gains.shape[0]], small.result[norm_gains.shape[0] :]
    residual = inputs.astype(F32).reshape(tokens, width)
    ffn1_norm, ffn1_normed, ffn1_scale = layer_norm(residual, gains[0])
    ffn1_hidden = after(ffn1_norm.astype(BF16), tables)
    follow(g2, g1)
    step(land=[g1])
    g1.operand = after(g1.operand, [gains])
    g1.go()
    step(land=[g2])
    follow(g2, g1)
    for _ in range(2):
        step(land=[g1], go=[g1])
        step(land=[g2])
        follow(g2, g1)
    w_attn_out, w_conv_in, w_conv_out, w_ffn2_in, w_ffn2_out = late_weights(*ready(g2))
    (w_ffn1_in,) = finish(g1)
    before_1 = dot(ffn1_hidden, w_ffn1_in)
    after_1 = (before_1 * jax.nn.sigmoid(before_1)).astype(BF16)
    (w_ffn1_out,) = finish(g2)
    first = residual + 0.5 * dot(after_1, w_ffn1_out)
    attn_norm, attn_normed, attn_scale = layer_norm(first, gains[1])
    attn_hidden = attn_norm.astype(BF16)
    packed = dot(attn_hidden, w_qkv)
    queries = packed[:, :width]
    keys = packed[:, width : 2 * width]
    queries = (queries * cosine + half_turn(queries) * sine).astype(BF16)
    keys = (keys * cosine + half_turn(keys) * sine).astype(BF16)
    values = packed[:, 2 * width :].astype(BF16)
    heads = Lane(
        heads_lane(
            plan,
            jnp.concatenate([to_groups(queries), to_groups(keys), to_groups(values)], axis=-1),
        )
    )

    def as_rows(x):
        x = x.reshape(wide, row_count, frames_here, group)
        return x.transpose(1, 0, 2, 3).reshape(row_count, frame_total, group)

    def as_blocks(x):
        x = x.reshape(row_count, wide, frames_here, group)
        return x.transpose(1, 0, 2, 3).reshape(wide, tokens, group)

    arrived = finish(heads)
    row_queries = as_rows(arrived[..., :group])
    row_keys = as_rows(arrived[..., group : 2 * group])
    row_values = as_rows(arrived[..., 2 * group :])
    mixed_rows, row_totals = attend(row_queries, row_keys, row_values, row_ids)
    heads = Lane(heads_lane(plan, as_blocks(mixed_rows)))
    mixed = from_groups(finish(heads))
    second = first + dot(mixed, w_attn_out)
    conv_norm, conv_normed, conv_scale = layer_norm(second, gains[2])
    conv_hidden = conv_norm.astype(BF16)
    gated = dot(conv_hidden, w_conv_in)
    gate_sig = jax.nn.sigmoid(gated[:, width:])
    glu = (gated[:, :width] * gate_sig).astype(BF16).reshape(row_count, frames_here, width)
    before, after_frames = neighbours(glu, half_width, 1)
    extended = jnp.concatenate(
        [before, glu, after_frames, jnp.zeros((row_count, 32 - 2 * half_width, width), BF16)],
        axis=1,
    )
    convolved = depthwise(extended, edge_ids, kernel).reshape(tokens, width)
    inner_out, inner_normed, inner_scale = layer_norm(convolved, gains[3])
    activated = (inner_out * jax.nn.sigmoid(inner_out)).astype(BF16)
    third = second + dot(activated, w_conv_out)
    ffn2_norm, ffn2_normed, ffn2_scale = layer_norm(third, gains[4])
    ffn2_hidden = ffn2_norm.astype(BF16)
    before_2 = dot(ffn2_hidden, w_ffn2_in)
    after_2 = (before_2 * jax.nn.sigmoid(before_2)).astype(BF16)
    fourth = third + 0.5 * dot(after_2, w_ffn2_out)
    final_out, final_normed, final_scale = layer_norm(fourth, gains[5])
    layer_out = final_out.astype(BF16).reshape(inputs.shape)

    def grads(left, right, small=None):
        return Lane(grad_lane(plan, *left, right, small))

    gradient, gain_final = norm_backward(
        cotangent.astype(F32).reshape(tokens, width), gains[5], final_normed, final_scale
    )
    branch = (0.5 * gradient).astype(BF16)
    r1 = grads(pick_columns(plan, after_2, orders), branch)
    r1.go()
    before_grad = (dot_back(branch, w_ffn2_out) * swish_slope(before_2)).astype(BF16)
    r2 = grads(pick(ffn2_hidden), before_grad)
    r2.go()
    step(land=[r1], go=[r1], since=[before_grad])
    input_grad, gain_ffn2 = norm_backward(
        dot_back(before_grad, w_ffn2_in), gains[4], ffn2_normed, ffn2_scale
    )
    gradient = gradient + input_grad
    conv_branch = after(gradient.astype(BF16), jax.tree.leaves(ready(r1)))
    r3 = grads(pick(activated), conv_branch)
    r3.go()
    act_grad = dot_back(conv_branch, w_conv_out) * swish_slope(inner_out)
    conv_grad, gain_inner = norm_backward(act_grad, gains[3], inner_normed, inner_scale)
    step(land=[r2], go=[r2], since=[conv_branch])
    kernel_terms, ext_grad = depthwise_back(
        extended,
        edge_ids,
        conv_grad.reshape(row_count, frames_here, width),
        kernel,
        jax.tree.leaves(ready(r1, r2)),
    )
    grad_kernel = jnp.sum(kernel_terms, axis=0)
    end = half_width + frames_here
    rims = ext_grad[:, :half_width], ext_grad[:, end : end + half_width]
    to_before, to_after = (rim.astype(BF16) for rim in rims)
    up = [(i, i + 1) for i in range(wide - 1)]
    from_before = lax.ppermute(to_after, "wide", up).astype(F32)
    from_after = lax.ppermute(to_before, "wide", [(j, i) for i, j in up]).astype(F32)
    middle = jnp.zeros((row_count, frames_here - 2 * half_width, width), F32)
    glu_grad = ext_grad[:, half_width:end] + jnp.concatenate(
        [from_before, middle, from_after], axis=1
    )
    glu_grad = glu_grad.reshape(tokens, width)
    gated_grad = jnp.concatenate(
        [glu_grad * gate_sig, glu_grad * gated[:, :width] * gate_sig * (1.0 - gate_sig)],
        axis=-1,
    ).astype(BF16)
    r4 = grads(pick(conv_hidden), gated_grad)
    r4.go()
    norm_grad, gain_conv = norm_backward(
        dot_back(gated_grad, w_conv_in), gains[2], conv_normed, conv_scale
    )
    gradient = gradient + norm_grad
    attn_branch = step(
        land=[r1, r3], go=[r1, r3], chain=gradient.astype(BF16), since=[kernel_terms]
    )
    head_grads = dot_back(attn_branch, w_attn_out).astype(BF16)
    heads = Lane(heads_lane(plan, to_groups(head_grads)))
    r5 = grads(pick(mixed), attn_branch)
    r5.go()
    step(go=[heads])
    step(land=[heads], go=[heads])
    step(land=[r2, r4], go=[r2, r4], since=ready(heads)[0])
    row_grads = as_rows(finish(heads))
    query_grad, key_grad, value_grad = attend_back(
        row_queries,
        row_keys,
        row_values,
        mixed_rows,
        row_grads,
        row_totals,
        row_ids,
        row_cosine,
        row_sine,
        jax.tree.leaves(ready(r2, r4)),
    )
    heads = Lane(
        heads_lane(
            plan,
            jnp.concatenate(
                [as_blocks(query_grad), as_blocks(key_grad), as_blocks(value_grad)], axis=-1
            ),
        )
    )
    step(go=[heads])
    step(land=[heads], go=[heads])
    step(land=[r1, r2, r3, r4, r5], go=[r3, r4, r5], since=ready(heads)[0])
    returned = finish(heads)
    returned = after(returned, jax.tree.leaves(ready(r1, r2, r3, r4, r5)))
    hold(r1, returned)
    hold(r2, returned)
    packed_grad = jnp.concatenate(
        [from_groups(returned[..., part * group : (part + 1) * group]) for part in range(3)],
        axis=-1,
    )
    packed_grad = lax.optimization_barrier(packed_grad)
    r6 = grads(pick(attn_hidden), packed_grad)
    r6.go()
    norm_grad, gain_attn = norm_backward(
        dot_back(packed_grad, w_qkv), gains[1], attn_normed, attn_scale
    )
    gradient = gradient + norm_grad
    branch = (0.5 * gradient).astype(BF16)
    branch = step(land=[r6], go=[r6], chain=branch)
    r7 = grads(pick_columns(plan, after_1, orders), branch)
    r7.go()
    before_grad = (dot_back(branch, w_ffn1_out) * swish_slope(before_1)).astype(BF16)
    before_grad = lax.optimization_barrier(before_grad)

    def small_sums():
        total = jnp.concatenate([grad_gains, grad_kernel], axis=0)
        total = jnp.dot(total, tree_pick.astype(F32), precision=HIGHEST)
        return total[:, : width // 2] + send(total[:, width // 2 :], plan.flip_pairs(plan.rows))

    before_grad = lax.optimization_barrier(before_grad)
    r8 = grads(pick(ffn1_hidden), before_grad, small_sums)
    r8.go()
    before_grad = step(land=[r7], go=[r7], chain=before_grad)
    input_grad, gain_ffn1 = norm_backward(
        dot_back(before_grad, w_ffn1_in), gains[0], ffn1_normed, ffn1_scale
    )
    gradient = gradient + input_grad
    grad_gains = jnp.stack([gain_ffn1, gain_attn, gain_conv, gain_inner, gain_ffn2, gain_final])
    step(land=[r8], go=[r8])
    step(land=[r1, r2, r3, r4, r5], go=[r3, r4, r5], since=[gradient])
    step(land=[r6], go=[r6])
    finish(r1, r2, r3, r4, r5, r6, r7, r8)
    grad_ffn1_in, small_shard = r8.result
    grad_ffn1_out, grad_qkv = r7.result, r6.result
    grad_attn_out, grad_conv_in, grad_conv_out = r5.result, r4.result, r3.result
    grad_ffn2_in, grad_ffn2_out = r2.result, r1.result
    shard_gains, shard_kernel = small_shard[: grad_gains.shape[0]], small_shard[grad_gains.shape[0] :]

    return (
        layer_out,
        gradient.astype(BF16).reshape(inputs.shape),
        grad_ffn1_in,
        grad_ffn1_out,
        grad_qkv,
        grad_attn_out,
        grad_conv_in,
        shard_kernel,
        grad_conv_out,
        grad_ffn2_in,
        grad_ffn2_out,
        shard_gains,
    )


def solution(mesh):
    frames = P("rows", "wide", None)
    split_rows = P(BOTH, None)
    split_columns = P(None, BOTH)
    weights = (split_rows,) * 5 + (split_columns,) + (split_rows,) * 3 + (split_columns,)
    return jax.shard_map(
        per_device,
        mesh=mesh,
        in_specs=(frames, P("rows", None)) + weights + (frames,),
        out_specs=(frames, frames) + weights,
        check_vma=False,
    )
```

```python
import functools

import jax
import jax.numpy as jnp
import numpy as np
from jax import lax
from jax.experimental import pallas as pl
from jax.experimental.pallas import tpu as pltpu
from jax.sharding import PartitionSpec as P

HEADS = 16
HEAD_DIM = 64
EPSILON = 1e-05
BOTH = ("wide", "rows")
F32 = jnp.float32
BF16 = jnp.bfloat16
HIGHEST = lax.Precision.HIGHEST
VMEM_LIMIT = 60 * 1024 * 1024


class Plan:
    def __init__(self, wide, rows):
        self.wide, self.rows, self.total = wide, rows, wide * rows
        self.far = [k * 2 * rows for k in range(1, wide // 2)]
        row_bits = [1 << b for b in range(rows.bit_length() - 1)]
        self.flips = (row_bits, row_bits[1:] + row_bits[:1])
        self.stages = len(row_bits)
        self.far_bits = [1 << b for b in range((wide // 2).bit_length() - 1)]
        self.blocks = self.total // 2
        far = [0]
        for bit in reversed(self.far_bits):
            far += [k | bit for k in far]
        self.table = [
            np.array(
                [
                    (k * 2 * rows) ^ sum(f for t, f in enumerate(flips) if p >> t & 1)
                    for p in range(1 << self.stages)
                    for k in far
                ],
                np.int32,
            )
            for flips in self.flips
        ]

    def halvings(self):
        near = [self.stage_pairs(t) for t in reversed(range(self.stages))]
        return near + [self.flip_pairs(bit * 2 * self.rows) for bit in self.far_bits]

    def core_of(self, index):
        return (index // self.rows) % 2

    def stage_pairs(self, stage):
        return [(i, i ^ self.flips[self.core_of(i)][stage]) for i in range(self.total)]

    def flip_pairs(self, flip):
        return [(i, i ^ flip) for i in range(self.total)]

    def orders(self):
        index = lax.axis_index(BOTH)
        core = self.core_of(index)
        table = jnp.stack([jnp.asarray(t) for t in self.table])
        own = index ^ jnp.take(table, core, axis=0)
        other = (index ^ self.rows) ^ jnp.take(table, 1 - core, axis=0)
        return own, other


def send(x, pairs):
    return lax.ppermute(x, BOTH, pairs)


def held(arrays):
    return [pl.BlockSpec(memory_space=pl.ANY)] * len(arrays)


def there(tokens, before=None):
    tokens = jax.tree.leaves((tokens, before))
    if not tokens:
        return None

    def kernel(*refs):
        refs[-1][0] = 1

    return pl.pallas_call(
        kernel,
        out_shape=jax.ShapeDtypeStruct((1,), jnp.int32),
        in_specs=held(tokens),
        out_specs=pl.BlockSpec(memory_space=pltpu.SMEM),
        cost_estimate=pl.CostEstimate(flops=0, transcendentals=0, bytes_accessed=0),
        name="there",
    )(*tokens)


def after(values, tokens, before=None):
    flag = there(tokens, before) if jax.tree.leaves(tokens) else before
    if flag is None or not jax.tree.leaves(values):
        return values
    flag = flag[0] > 0
    return jax.tree.map(lambda x: jnp.where(flag, x, jnp.zeros((), x.dtype)), values)


class Lane:
    def __init__(self, steps):
        self.steps, self.result, self.arriving = steps, None, None
        self.operand, self.pairs = next(steps)

    def go(self):
        if isinstance(self.pairs[0], list):
            self.arriving = [send(x, pairs) for x, pairs in zip(self.operand, self.pairs)]
        else:
            self.arriving = jax.tree.map(lambda x: send(x, self.pairs), self.operand)

    def landed(self, arrived):
        self.arriving = None
        try:
            self.operand, self.pairs = self.steps.send(arrived)
        except StopIteration as stop:
            self.operand, self.result = None, stop.value


def step(land=(), go=(), chain=(), since=()):
    land = [lane for lane in land if lane.arriving is not None]
    flag = there(list(since)) if since else None
    for lane in land:
        lane.landed(after(lane.arriving, [], flag))
    if jax.tree.leaves(chain):
        chain = after(chain, jax.tree.leaves(ready(*land)))
    for lane in go:
        if lane.operand is not None and lane.arriving is None:
            lane.go()
    return chain


def hold(lane, *tokens):
    if lane.operand is not None:
        lane.operand = after(lane.operand, list(tokens))
        lane.go()


def waited(*lanes):
    return [lane.arriving for lane in lanes if lane.arriving is not None]


def ready(*lanes):
    return [lane.operand for lane in lanes if lane.operand is not None]


def finish(*lanes, since=()):
    while any(lane.operand is not None for lane in lanes):
        for lane in lanes:
            step(land=[lane], go=[lane], since=since)
    return lanes[0].result


def gather_lane(plan, shard, finish):
    held = shard[None]
    for bit in reversed(plan.far_bits):
        pairs = plan.flip_pairs(bit * 2 * plan.rows)
        arrived = yield held, pairs
        held = jnp.concatenate([held, arrived], axis=0)
    for stage in range(plan.stages - 1):
        held = jnp.concatenate([held, (yield held, plan.stage_pairs(stage))], axis=0)
    last = yield held, plan.stage_pairs(plan.stages - 1)
    from_core = yield [held, last], plan.flip_pairs(plan.rows)
    return finish([held, last, *from_core])


def grad_lane(plan, lefts, rights, split=0):
    others = [other for _, other in lefts]
    if len(rights) > 1:
        others, sent = [jnp.concatenate(others, axis=1)], [jnp.concatenate(rights, axis=1)]
    else:
        sent = rights
    arrived = yield [others[0], sent[0]], plan.flip_pairs(plan.rows)
    columns = np.cumsum([0] + [right.shape[1] for right in rights])
    size = lefts[0][0].shape[1]
    left = [
        jnp.concatenate([own, arrived[0][:, k * size : (k + 1) * size]], axis=0)
        for k, (own, _) in enumerate(lefts)
    ]
    both = [
        jnp.concatenate([right, arrived[1][:, columns[k] : columns[k + 1]]], axis=0)
        for k, right in enumerate(rights)
    ]
    left, both = lax.optimization_barrier((left, both))

    def products(first, last):
        parts = [
            dot_over_frames(one[:, size * first // 4 : size * last // 4], other).astype(BF16)
            for one, other in zip(left, both)
        ]
        return jnp.concatenate(parts, axis=1) if len(parts) > 1 else parts[0]

    away, kept = None, None
    halvings = plan.halvings()
    for count, pairs in enumerate(halvings):
        if count == 0:
            parts = (products(3, 4), products(2, 3)) if split else (products(2, 4),)
        elif count < split:
            half, quarter = kept.shape[0] // 2, kept.shape[0] // 4
            parts = (
                (kept[half + quarter :].astype(F32) + onward[quarter:].astype(F32)).astype(BF16),
                (kept[half : half + quarter].astype(F32) + onward[:quarter].astype(F32)).astype(BF16),
            )
        else:
            half = kept.shape[0] // 2
            parts = ((kept[half:].astype(F32) + onward.astype(F32)).astype(BF16),)
        if count == 0:
            kept = products(0, 2)
        else:
            kept = (kept[:half].astype(F32) + stay.astype(F32)).astype(BF16)
        if len(parts) == 2:
            onward, stay = yield list(parts), pairs
        else:
            arrived = yield parts[0], pairs
            onward, stay = arrived[arrived.shape[0] // 2 :], arrived[: arrived.shape[0] // 2]
    total = kept.astype(F32) + arrived.astype(F32)
    return [total[:, columns[k] : columns[k + 1]] for k in range(len(rights))]


def small_grad_lane(plan, both):
    half = both.shape[1] // 2
    total = both[:, :half] + (yield both[:, half:], plan.flip_pairs(plan.rows))
    for pairs in plan.halvings():
        half = total.shape[1] // 2
        total = total[:, :half] + (yield total[:, half:], pairs)
    return total


def heads_lane(plan, x):
    sent = x.reshape(plan.wide // 2, 2, *x.shape[1:])
    from_core = yield sent[:, 1], plan.flip_pairs(plan.rows)
    pair = jnp.stack([sent[:, 0], from_core], axis=1)
    arrived = yield (
        [pair[k] for k in range(1, plan.wide // 2)],
        [plan.flip_pairs(far) for far in plan.far],
    )
    return jnp.stack([pair[0], *arrived]).reshape(x.shape)


def assemble(plan, pieces, shapes, orders):
    half = plan.blocks // 2
    width = pieces[0].shape[-1]
    index = jnp.concatenate(orders)
    if any(rows % 16 for rows, _ in shapes):
        stacked = jnp.concatenate(pieces, axis=0)
        place = jnp.zeros((plan.total,), jnp.int32).at[index].set(jnp.arange(plan.total))
        stacked = jnp.take(stacked, place, axis=0)
        outs, start = [], 0
        for rows, columns in shapes:
            parts = []
            for _ in range(columns // width):
                parts.append(stacked[:, start : start + rows].reshape(-1, width))
                start += rows
            outs.append(jnp.concatenate(parts, axis=1))
        return outs

    def kernel(order, *refs):
        sources, outs = refs[:4], refs[4:-3]
        held, in_sems, out_sems = refs[-3:]
        loads = [
            pltpu.make_async_copy(sources[which], held.at[which], in_sems.at[which])
            for which in range(4)
        ]
        for load in loads:
            load.start()
        for which in range(4):
            loads[which].wait()
            for place in range(half):
                block = order[which * half + place]
                start = 0
                for out, (rows, columns) in enumerate(shapes):
                    for part in range(columns // width):
                        pltpu.make_async_copy(
                            held.at[which, place, pl.ds(start, rows)],
                            outs[out].at[
                                pl.ds(pl.multiple_of(block * rows, rows), rows),
                                pl.ds(part * width, width),
                            ],
                            out_sems.at[out],
                        ).start()
                        start += rows
        for out in range(len(shapes)):
            pltpu.make_async_copy(outs[out], outs[out], out_sems.at[out]).wait()

    return pl.pallas_call(
        kernel,
        out_shape=[
            jax.ShapeDtypeStruct((rows * plan.total, columns), BF16) for rows, columns in shapes
        ],
        in_specs=[pl.BlockSpec(memory_space=pltpu.SMEM)] + [pl.BlockSpec(memory_space=pl.ANY)] * 4,
        out_specs=[pl.BlockSpec(memory_space=pl.ANY)] * len(shapes),
        scratch_shapes=[
            pltpu.VMEM((4,) + pieces[0].shape, BF16),
            pltpu.SemaphoreType.DMA((4,)),
            pltpu.SemaphoreType.DMA((len(shapes),)),
        ],
        compiler_params=pltpu.CompilerParams(vmem_limit_bytes=24 * 1024 * 1024),
        cost_estimate=pl.CostEstimate(
            flops=0, transcendentals=0, bytes_accessed=8 * pieces[0].size * 2
        ),
        name="assemble",
    )(index, *pieces)


def pick_columns(plan, x, orders):
    index = jnp.concatenate(orders)
    length, columns = x.shape
    size = columns // plan.total
    if size % 128:
        split = jnp.take(x.reshape(length, plan.total, size), index, axis=1)
        split = split.reshape(length, columns)
        return split[:, : columns // 2], split[:, columns // 2 :]

    def kernel(order, source, first, second):
        for place in range(plan.total):
            out = (first, second)[place // plan.blocks]
            start = pl.multiple_of(order[place] * size, size)
            out[:, pl.ds((place % plan.blocks) * size, size)] = source[:, pl.ds(start, size)]

    whole = pl.BlockSpec(memory_space=pltpu.VMEM)
    return pl.pallas_call(
        kernel,
        out_shape=[jax.ShapeDtypeStruct((length, columns // 2), x.dtype)] * 2,
        in_specs=[pl.BlockSpec(memory_space=pltpu.SMEM), whole],
        out_specs=[whole] * 2,
        compiler_params=pltpu.CompilerParams(vmem_limit_bytes=16 * 1024 * 1024),
        cost_estimate=pl.CostEstimate(
            flops=0, transcendentals=0, bytes_accessed=4 * x.size
        ),
        name="pick_columns",
    )(index, x)


def dot(left, right):
    return jnp.dot(left, right, preferred_element_type=F32)


def dot_back(left, right):
    return lax.dot_general(left, right, (((1,), (1,)), ((), ())), preferred_element_type=F32)


def dot_over_frames(left, right):
    return lax.dot_general(left, right, (((0,), (0,)), ((), ())), preferred_element_type=F32)


def head_lanes(size, head):
    lane = lax.broadcasted_iota(jnp.int32, (1, size), 1)
    return (lane >= head * HEAD_DIM) & (lane < (head + 1) * HEAD_DIM)


def attend_kernel(q_ref, k_ref, v_ref, idq_ref, idk_ref, o_ref, total_ref):
    size = q_ref.shape[-1]
    query, keys, values = q_ref[0] * HEAD_DIM**-0.5, k_ref[0], v_ref[0]
    same = idq_ref[0] == idk_ref[0]
    mixed = jnp.zeros(query.shape, F32)
    totals = []
    for head in range(size // HEAD_DIM):
        lanes = head_lanes(size, head)
        scores = lax.dot_general(
            jnp.where(lanes, query, 0), keys, (((1,), (1,)), ((), ())), preferred_element_type=F32
        )
        scores = jnp.where(same, scores, -1e30)
        most = jnp.max(scores, axis=-1, keepdims=True)
        unnormed = jnp.exp(scores - most)
        total = jnp.sum(unnormed, axis=-1, keepdims=True)
        probs = (unnormed * (1.0 / total)).astype(BF16)
        mixed += jnp.dot(probs, jnp.where(lanes, values, 0), preferred_element_type=F32)
        totals.append(most + jnp.log(total))
    o_ref[0] = mixed.astype(BF16)
    total_ref[0] = jnp.concatenate(totals, axis=1)


def attend_back_kernel(
    q_ref, k_ref, v_ref, o_ref, do_ref, total_ref, idq_ref, idk_ref, cq_ref, sq_ref, ck_ref,
    sk_ref, turn_ref, dq_ref, dk_ref, dv_ref, dk_sum, dv_sum,
):
    step = pl.program_id(1)
    size = q_ref.shape[-1]
    scale = HEAD_DIM**-0.5
    query, keys, values, grads = q_ref[0] * scale, k_ref[0], v_ref[0], do_ref[0]
    different = idk_ref[0] != idq_ref[0]
    product = grads.astype(F32) * o_ref[0].astype(F32)

    @pl.when(step == 0)
    def _():
        dk_sum[...] = jnp.zeros_like(dk_sum)
        dv_sum[...] = jnp.zeros_like(dv_sum)

    turned_sum = jnp.zeros((size, query.shape[0]), F32)
    for head in range(size // HEAD_DIM):
        lanes = head_lanes(size, head)
        one_query = jnp.where(lanes, query, 0)
        one_grad = jnp.where(lanes, grads, 0)
        delta = lax.dot_general(
            jnp.where(lanes, jnp.ones((8, size), F32), 0.0),
            product,
            (((1,), (1,)), ((), ())),
            precision=HIGHEST,
            preferred_element_type=F32,
        )[:1]
        scores = lax.dot_general(
            keys, one_query, (((1,), (1,)), ((), ())), preferred_element_type=F32
        )
        probs = jnp.exp(jnp.where(different, -1e30, scores - total_ref[0, head : head + 1]))
        prob_grads = lax.dot_general(
            values, one_grad, (((1,), (1,)), ((), ())), preferred_element_type=F32
        )
        score_grads = (probs * (prob_grads - delta)).astype(BF16)
        dk_sum[...] += jnp.dot(score_grads, one_query, preferred_element_type=F32)
        dv_sum[...] += jnp.dot(probs.astype(BF16), one_grad, preferred_element_type=F32)
        turned_sum += dot_over_frames(jnp.where(lanes, keys, 0), score_grads)

    def turned(grad, cosine, sine):
        partner = jnp.dot(grad, turn_ref[...], precision=HIGHEST, preferred_element_type=F32)
        return (grad * cosine + partner * sine).astype(BF16)

    dq_ref[0] = turned(turned_sum.T * scale, cq_ref[0], sq_ref[0])

    @pl.when(step == pl.num_programs(1) - 1)
    def _():
        dk_ref[0] = turned(dk_sum[...], ck_ref[0], sk_ref[0])
        dv_ref[0] = dv_sum[...].astype(BF16)


def attend(query, keys, values, ids, tokens=()):
    rows, length, size = query.shape
    tile = 256
    heads = size // HEAD_DIM
    whole = pl.BlockSpec((1, length, size), lambda r, t: (r, 0, 0))
    part = pl.BlockSpec((1, tile, size), lambda r, t: (r, t, 0))
    return pl.pallas_call(
        lambda *refs: attend_kernel(*refs[:5], *refs[5 + len(tokens) :]),
        out_shape=[
            jax.ShapeDtypeStruct(query.shape, BF16),
            jax.ShapeDtypeStruct((rows, length, heads), F32),
        ],
        grid=(rows, length // tile),
        in_specs=[
            part,
            whole,
            whole,
            pl.BlockSpec((1, tile, 1), lambda r, t: (r, t, 0)),
            pl.BlockSpec((1, 1, length), lambda r, t: (r, 0, 0)),
            *held(tokens),
        ],
        out_specs=[part, pl.BlockSpec((1, tile, heads), lambda r, t: (r, t, 0))],
        compiler_params=pltpu.CompilerParams(vmem_limit_bytes=VMEM_LIMIT),
        name="attend",
    )(query, keys, values, ids[:, :, None], ids[:, None, :], *tokens)


def attend_back(query, keys, values, mixed, grads, totals, ids, cosine, sine, tokens=()):
    rows, length, size = query.shape
    tile = 256
    heads = size // HEAD_DIM
    whole = pl.BlockSpec((1, length, size), lambda r, t: (r, 0, 0))
    part = pl.BlockSpec((1, tile, size), lambda r, t: (r, t, 0))
    lane = np.arange(size)
    turn = jnp.asarray((lane[:, None] == (lane ^ (HEAD_DIM // 2))[None, :]).astype(np.float32))
    return pl.pallas_call(
        lambda *refs: attend_back_kernel(*refs[:13], *refs[13 + len(tokens) :]),
        out_shape=[jax.ShapeDtypeStruct(query.shape, BF16)] * 3,
        grid=(rows, length // tile),
        in_specs=[
            part,
            whole,
            whole,
            part,
            part,
            pl.BlockSpec((1, heads, tile), lambda r, t: (r, 0, t)),
            pl.BlockSpec((1, 1, tile), lambda r, t: (r, 0, t)),
            pl.BlockSpec((1, length, 1), lambda r, t: (r, 0, 0)),
            part,
            part,
            whole,
            whole,
            pl.BlockSpec((size, size), lambda r, t: (0, 0)),
            *held(tokens),
        ],
        out_specs=[part, whole, whole],
        scratch_shapes=[pltpu.VMEM((length, size), F32)] * 2,
        compiler_params=pltpu.CompilerParams(vmem_limit_bytes=VMEM_LIMIT),
        name="attend_back",
    )(
        query, keys, values, mixed, grads, totals.transpose(0, 2, 1), ids[:, None, :],
        ids[:, :, None], cosine, sine, cosine, sine, turn, *tokens,
    )


def set_masks(ids_ref, ids, masks, count):
    ids[...] = jnp.broadcast_to(ids_ref[0], ids.shape)
    here = ids[pl.ds(masks.shape[0] // 2, count)]
    for tap in range(masks.shape[0]):
        masks[tap] = jnp.where(ids[pl.ds(tap, count)] == here, 1.0, 0.0)


def conv_kernel(ext_ref, ids_ref, taps_ref, out_ref, frames, ids, masks):
    count, taps = out_ref.shape[1], taps_ref.shape[0]

    @pl.when(pl.program_id(1) == 0)
    def _():
        set_masks(ids_ref, ids, masks, count)

    frames[...] = ext_ref[0].astype(F32)
    total = jnp.zeros((count, frames.shape[1]), F32)
    for odd in range(8):
        shifted = frames[pl.ds(odd, frames.shape[0] - 8)]
        for tap in range(odd, taps, 8):
            part = shifted[tap - odd : tap - odd + count]
            total += part * masks[tap] * taps_ref[tap : tap + 1]
    out_ref[0] = total


def conv_back_kernel(
    ext_ref, ids_ref, grad_ref, taps_ref, dtaps_ref, dext_ref, frames, ids, masks, total, some
):
    count, taps = grad_ref.shape[1], taps_ref.shape[0]

    @pl.when(pl.program_id(1) == 0)
    def _():
        set_masks(ids_ref, ids, masks, count)

    frames[...] = ext_ref[0].astype(F32)
    grad = grad_ref[0]
    total[...] = jnp.zeros_like(total)
    rows = [None] * taps
    for odd in range(8):
        shifted = frames[pl.ds(odd, frames.shape[0] - 8)]
        some[...] = jnp.zeros_like(some)
        for tap in range(odd, taps, 8):
            kept = grad * masks[tap]
            rows[tap] = jnp.sum(shifted[tap - odd : tap - odd + count] * kept, axis=0, keepdims=True)
            some[pl.ds(tap - odd, count)] += kept * taps_ref[tap : tap + 1]
        total[pl.ds(odd, some.shape[0])] += some[...]
    dext_ref[0] = total[...]
    dtaps_ref[0] = jnp.concatenate(rows, axis=0)


def depthwise(extended, ids, taps, tokens=()):
    rows, padded, width = extended.shape
    count = padded - 32
    block = 128
    return pl.pallas_call(
        lambda *refs: conv_kernel(*refs[:3], *refs[3 + len(tokens) :]),
        out_shape=jax.ShapeDtypeStruct((rows, count, width), F32),
        grid=(rows, width // block),
        in_specs=[
            pl.BlockSpec((1, padded, block), lambda r, c: (r, 0, c)),
            pl.BlockSpec((1, padded, 1), lambda r, c: (r, 0, 0)),
            pl.BlockSpec((taps.shape[0], block), lambda r, c: (0, c)),
            *held(tokens),
        ],
        out_specs=pl.BlockSpec((1, count, block), lambda r, c: (r, 0, c)),
        scratch_shapes=[pltpu.VMEM((padded, block), F32)] * 2
        + [pltpu.VMEM((taps.shape[0], count, block), F32)],
        compiler_params=pltpu.CompilerParams(vmem_limit_bytes=16 * 1024 * 1024),
        name="depthwise",
    )(extended, ids, taps, *tokens)


def depthwise_back(extended, ids, grad, taps, tokens=()):
    rows, padded, width = extended.shape
    count = padded - 32
    block = 128
    return pl.pallas_call(
        lambda *refs: conv_back_kernel(*refs[:4], *refs[4 + len(tokens) :]),
        out_shape=[
            jax.ShapeDtypeStruct((rows, taps.shape[0], width), F32),
            jax.ShapeDtypeStruct((rows, padded, width), F32),
        ],
        grid=(rows, width // block),
        in_specs=[
            pl.BlockSpec((1, padded, block), lambda r, c: (r, 0, c)),
            pl.BlockSpec((1, padded, 1), lambda r, c: (r, 0, 0)),
            pl.BlockSpec((1, count, block), lambda r, c: (r, 0, c)),
            pl.BlockSpec((taps.shape[0], block), lambda r, c: (0, c)),
            *held(tokens),
        ],
        out_specs=[
            pl.BlockSpec((1, taps.shape[0], block), lambda r, c: (r, 0, c)),
            pl.BlockSpec((1, padded, block), lambda r, c: (r, 0, c)),
        ],
        scratch_shapes=[pltpu.VMEM((padded, block), F32)] * 2
        + [
            pltpu.VMEM((taps.shape[0], count, block), F32),
            pltpu.VMEM((padded, block), F32),
            pltpu.VMEM((padded - 8, block), F32),
        ],
        compiler_params=pltpu.CompilerParams(vmem_limit_bytes=16 * 1024 * 1024),
        name="depthwise_back",
    )(extended, ids, grad, taps, *tokens)


def segment_info(lengths, frame_total):
    segment_end = jnp.cumsum(lengths, axis=-1, dtype=jnp.int32)
    frame_index = jnp.arange(frame_total, dtype=jnp.int32)
    passed = (frame_index[None, None, :] >= segment_end[:, :, None]).astype(jnp.int32)
    segment_ids = jnp.sum(passed, axis=1, dtype=jnp.int32)
    seg_starts = jnp.sum(passed * lengths[:, :, None], axis=1, dtype=jnp.int32)
    return (segment_ids, frame_index[None, :] - seg_starts)


def layer_norm(values, gain_row):
    centred = values - jnp.mean(values, axis=-1, keepdims=True)
    inv_scale = lax.rsqrt(jnp.mean(centred * centred, axis=-1, keepdims=True) + EPSILON)
    normed = centred * inv_scale
    return (normed * gain_row, normed, inv_scale)


def norm_backward(gradient, gain_row, normed, inv_scale):
    scaled = gradient * gain_row
    gain_grad = jnp.sum(gradient * normed, axis=0)
    centred_mean = jnp.mean(scaled, axis=-1, keepdims=True)
    product_mean = jnp.mean(scaled * normed, axis=-1, keepdims=True)
    return (inv_scale * (scaled - centred_mean - normed * product_mean), gain_grad)


def swish_slope(values):
    gate_sig = jax.nn.sigmoid(values)
    return gate_sig * (1.0 + values * (1.0 - gate_sig))


def neighbours(x, width, axis):
    size, length = lax.axis_size("wide"), x.shape[axis]
    up = [(i, i + 1) for i in range(size - 1)]
    before = lax.ppermute(lax.slice_in_dim(x, length - width, length, axis=axis), "wide", up)
    after = lax.ppermute(
        lax.slice_in_dim(x, 0, width, axis=axis), "wide", [(j, i) for i, j in up]
    )
    return before, after


def half_turn(values):
    half = HEAD_DIM // 2
    lane = lax.broadcasted_iota(jnp.int32, (1, values.shape[-1]), 1) % HEAD_DIM
    ahead = jnp.roll(values, -half, axis=-1)
    behind = jnp.roll(values, half, axis=-1)
    return jnp.where(lane < half, -ahead, behind)


def per_device(
    inputs,
    lengths,
    ffn1_in,
    ffn1_out,
    attn_qkv,
    attn_out,
    conv_in,
    depth_kernel,
    conv_out,
    ffn2_in,
    ffn2_out,
    norm_gains,
    cotangent,
):
    wide, rows = lax.axis_size("wide"), lax.axis_size("rows")
    plan = Plan(wide, rows)
    row_count, frames_here, width = inputs.shape
    tokens = row_count * frames_here
    frame_total = frames_here * wide
    taps = depth_kernel.shape[0]
    half_width = taps // 2
    me = lax.axis_index("wide")
    orders = plan.orders()
    segment_ids, position = segment_info(lengths, frame_total)

    def packed_shards(shards):
        parts = []
        for shard in shards:
            for column in range(0, shard.shape[1], width):
                parts.append(shard[:, column : column + width])
        return jnp.concatenate(parts, axis=0) if len(parts) > 1 else parts[0]

    def weights_lane(*shards):
        shapes = [shard.shape for shard in shards]
        return Lane(
            gather_lane(
                plan, packed_shards(shards), lambda held: assemble(plan, held, shapes, orders)
            )
        )

    def small_lane(small):
        flip = 1
        while flip < plan.total:
            small = jnp.concatenate([small, (yield small, plan.flip_pairs(flip))], axis=1)
            flip *= 2
        return dot_back(small, small_pick.astype(BF16))

    feature = jnp.arange(width, dtype=jnp.int32)
    block = width // plan.total
    small_source = (feature // block ^ lax.axis_index(BOTH)) * block + feature % block
    small_pick = feature[:, None] == small_source[None, :]
    small = Lane(small_lane(jnp.concatenate([norm_gains, depth_kernel], axis=0)))
    g1, g2 = weights_lane(ffn1_in), weights_lane(ffn1_out)
    w_qkv = lax.all_gather(attn_qkv, BOTH, axis=0, tiled=True)
    wides = (attn_out, conv_in, conv_out)
    middle = lax.all_gather(jnp.concatenate(wides, axis=1), BOTH, axis=0, tiled=True)
    cuts = np.cumsum([0] + [shard.shape[1] for shard in wides])
    w_attn_out, w_conv_in, w_conv_out = (
        middle[:, start:stop] for start, stop in zip(cuts[:-1], cuts[1:])
    )
    w_ffn2_in = lax.all_gather(ffn2_in, BOTH, axis=0, tiled=True)
    g4 = weights_lane(ffn2_out)

    source = jnp.repeat(jnp.concatenate(orders), block) * block + feature % block
    tree_pick = (feature[:, None] == source[None, :]).astype(BF16)
    group = width // wide
    head_source = (feature // group ^ me) * group + feature % group
    head_pick = (feature[:, None] == head_source[None, :]).astype(BF16)

    def pick(x):
        both = dot(x, tree_pick).astype(BF16)
        return both[:, : width // 2], both[:, width // 2 :]

    def to_groups(x):
        return dot(x, head_pick).astype(BF16).reshape(tokens, wide, group).transpose(1, 0, 2)

    def from_groups(x):
        return dot_back(x.transpose(1, 0, 2).reshape(tokens, width), head_pick).astype(BF16)

    offset = me * frames_here
    padded_ids = jnp.pad(segment_ids, ((0, 0), (half_width, 32 - half_width)), constant_values=-1)
    edge_ids = lax.dynamic_slice_in_dim(padded_ids, offset, frames_here + 32, 1)
    edge_ids = edge_ids.astype(F32)[:, :, None]
    local_position = lax.dynamic_slice_in_dim(position, offset, frames_here, 1)
    by_device = jnp.arange(wide, dtype=jnp.int32) ^ me

    def row_order(x):
        x = x.reshape(row_count, wide, frames_here)
        return jnp.take(x, by_device, axis=1).reshape(row_count, frame_total)

    row_ids, row_position = row_order(segment_ids), row_order(position)

    def rotation(at, size):
        lane = jnp.arange(size, dtype=jnp.int32) % HEAD_DIM
        frequency = jnp.power(
            10000.0, -2.0 * (lane % (HEAD_DIM // 2)).astype(F32) / HEAD_DIM
        )
        angles = at.astype(F32)[..., None] * frequency
        sign = jnp.where(lane < HEAD_DIM // 2, 1.0, -1.0)
        return jnp.cos(angles), jnp.sin(angles), sign

    cosine, sine, _ = rotation(local_position.reshape(tokens), HEAD_DIM)
    cosine = jnp.tile(cosine, (1, HEADS))
    sine = jnp.tile(sine, (1, HEADS))
    row_cosine, row_sine, sign = rotation(row_position, group)
    row_sine = row_sine * sign

    tables = (row_cosine, row_sine, cosine, sine, edge_ids)
    def follow(lane, leader):
        lane.operand = after(lane.operand, jax.tree.leaves(ready(leader)))
        lane.go()

    step(go=[g1, small])
    for _ in range(3):
        step(land=[small], go=[small])
    step(land=[g1, small], go=[small])
    follow(g1, small)
    finish(small)
    gains, kernel = small.result[: norm_gains.shape[0]], small.result[norm_gains.shape[0] :]
    residual = inputs.astype(F32).reshape(tokens, width)
    ffn1_norm, ffn1_normed, ffn1_scale = layer_norm(residual, gains[0])
    ffn1_hidden = after(ffn1_norm.astype(BF16), tables)
    follow(g2, g1)
    step(land=[g1])
    g1.operand = after(g1.operand, [gains])
    g1.go()
    step(land=[g2])
    follow(g2, g1)
    for _ in range(2):
        step(land=[g1], go=[g1])
        step(land=[g2])
        follow(g2, g1)
    follow(g4, g2)
    (w_ffn1_in,) = finish(g1)
    before_1 = dot(ffn1_hidden, w_ffn1_in)
    after_1 = (before_1 * jax.nn.sigmoid(before_1)).astype(BF16)
    (w_ffn1_out,) = finish(g2)
    first = residual + 0.5 * dot(after_1, w_ffn1_out)
    attn_norm, attn_normed, attn_scale = layer_norm(first, gains[1])
    attn_hidden = attn_norm.astype(BF16)
    packed = dot(attn_hidden, w_qkv)
    step(land=[g4], go=[g4], since=[packed])
    queries = packed[:, :width]
    keys = packed[:, width : 2 * width]
    queries = (queries * cosine + half_turn(queries) * sine).astype(BF16)
    keys = (keys * cosine + half_turn(keys) * sine).astype(BF16)
    values = packed[:, 2 * width :].astype(BF16)
    heads = Lane(
        heads_lane(
            plan,
            jnp.concatenate([to_groups(queries), to_groups(keys), to_groups(values)], axis=-1),
        )
    )

    def as_rows(x):
        x = x.reshape(wide, row_count, frames_here, group)
        return x.transpose(1, 0, 2, 3).reshape(row_count, frame_total, group)

    def as_blocks(x):
        x = x.reshape(row_count, wide, frames_here, group)
        return x.transpose(1, 0, 2, 3).reshape(wide, tokens, group)

    step(go=[heads])
    step(land=[heads], go=[heads])
    step(land=[g4], since=ready(heads)[0])
    arrived = finish(heads)
    hold(g4, arrived)
    row_queries = as_rows(arrived[..., :group])
    row_keys = as_rows(arrived[..., group : 2 * group])
    row_values = as_rows(arrived[..., 2 * group :])
    mixed_rows, row_totals = attend(row_queries, row_keys, row_values, row_ids)
    heads = Lane(heads_lane(plan, as_blocks(mixed_rows)))
    step(go=[heads])
    step(land=[heads], go=[heads])
    step(land=[g4], go=[g4], since=ready(heads)[0])
    mixed = from_groups(finish(heads))
    second = first + dot(mixed, w_attn_out)
    conv_norm, conv_normed, conv_scale = layer_norm(second, gains[2])
    conv_hidden = conv_norm.astype(BF16)
    gated = dot(conv_hidden, w_conv_in)
    gate_sig = jax.nn.sigmoid(gated[:, width:])
    glu = (gated[:, :width] * gate_sig).astype(BF16).reshape(row_count, frames_here, width)
    before, after_frames = neighbours(glu, half_width, 1)
    extended = jnp.concatenate(
        [before, glu, after_frames, jnp.zeros((row_count, 32 - 2 * half_width, width), BF16)],
        axis=1,
    )
    step(land=[g4], go=[g4], since=[gate_sig])
    convolved = depthwise(extended, edge_ids, kernel).reshape(tokens, width)
    inner_out, inner_normed, inner_scale = layer_norm(convolved, gains[3])
    activated = (inner_out * jax.nn.sigmoid(inner_out)).astype(BF16)
    third = second + dot(activated, w_conv_out)
    ffn2_norm, ffn2_normed, ffn2_scale = layer_norm(third, gains[4])
    ffn2_hidden = ffn2_norm.astype(BF16)
    before_2 = dot(ffn2_hidden, w_ffn2_in)
    after_2 = (before_2 * jax.nn.sigmoid(before_2)).astype(BF16)
    (w_ffn2_out,) = finish(g4)
    fourth = third + 0.5 * dot(after_2, w_ffn2_out)
    final_out, final_normed, final_scale = layer_norm(fourth, gains[5])
    layer_out = final_out.astype(BF16).reshape(inputs.shape)

    def grads(*pairs, split=0):
        lefts, rights = [left for left, _ in pairs], [right for _, right in pairs]
        return Lane(grad_lane(plan, lefts, rights, split))

    gradient, gain_final = norm_backward(
        cotangent.astype(F32).reshape(tokens, width), gains[5], final_normed, final_scale
    )
    branch = (0.5 * gradient).astype(BF16)
    r1 = grads((pick_columns(plan, after_2, orders), branch))
    r1.go()
    before_grad = (dot_back(branch, w_ffn2_out) * swish_slope(before_2)).astype(BF16)
    r2 = grads((pick(ffn2_hidden), before_grad))
    r2.go()
    step(land=[r1], go=[r1])
    input_grad, gain_ffn2 = norm_backward(
        dot_back(before_grad, w_ffn2_in), gains[4], ffn2_normed, ffn2_scale
    )
    gradient = gradient + input_grad
    conv_branch = after(gradient.astype(BF16), jax.tree.leaves(ready(r1)))
    act_grad = dot_back(conv_branch, w_conv_out) * swish_slope(inner_out)
    conv_grad, gain_inner = norm_backward(act_grad, gains[3], inner_normed, inner_scale)
    step(land=[r2], go=[r2])
    kernel_terms, ext_grad = depthwise_back(
        extended,
        edge_ids,
        conv_grad.reshape(row_count, frames_here, width),
        kernel,
        jax.tree.leaves(ready(r1, r2)),
    )
    grad_kernel = jnp.sum(kernel_terms, axis=0)
    end = half_width + frames_here
    rims = ext_grad[:, :half_width], ext_grad[:, end : end + half_width]
    to_before, to_after = (rim.astype(BF16) for rim in rims)
    up = [(i, i + 1) for i in range(wide - 1)]
    from_before = lax.ppermute(to_after, "wide", up).astype(F32)
    from_after = lax.ppermute(to_before, "wide", [(j, i) for i, j in up]).astype(F32)
    middle = jnp.zeros((row_count, frames_here - 2 * half_width, width), F32)
    glu_grad = ext_grad[:, half_width:end] + jnp.concatenate(
        [from_before, middle, from_after], axis=1
    )
    glu_grad = glu_grad.reshape(tokens, width)
    gated_grad = jnp.concatenate(
        [glu_grad * gate_sig, glu_grad * gated[:, :width] * gate_sig * (1.0 - gate_sig)],
        axis=-1,
    ).astype(BF16)
    norm_grad, gain_conv = norm_backward(
        dot_back(gated_grad, w_conv_in), gains[2], conv_normed, conv_scale
    )
    gradient = gradient + norm_grad
    attn_branch = gradient.astype(BF16)
    head_grads = dot_back(attn_branch, w_attn_out).astype(BF16)
    heads = Lane(heads_lane(plan, to_groups(head_grads)))
    r3 = grads(
        (pick(activated), conv_branch), (pick(conv_hidden), gated_grad), (pick(mixed), attn_branch)
    )
    step(go=[heads, r3])
    step(land=[heads], go=[heads])
    step(land=[r1, r3], go=[r1, r3], since=ready(heads)[0])
    row_grads = as_rows(finish(heads))
    query_grad, key_grad, value_grad = attend_back(
        row_queries,
        row_keys,
        row_values,
        mixed_rows,
        row_grads,
        row_totals,
        row_ids,
        row_cosine,
        row_sine,
        jax.tree.leaves(ready(r1, r3)),
    )
    heads = Lane(
        heads_lane(
            plan,
            jnp.concatenate(
                [as_blocks(query_grad), as_blocks(key_grad), as_blocks(value_grad)], axis=-1
            ),
        )
    )
    step(go=[heads])
    step(land=[heads], go=[heads])
    step(land=[r1, r2, r3], go=[r2, r3], since=ready(heads)[0])
    returned = finish(heads)
    returned = after(returned, jax.tree.leaves(ready(r1, r2, r3)))
    hold(r1, returned)
    packed_grad = jnp.concatenate(
        [from_groups(returned[..., part * group : (part + 1) * group]) for part in range(3)],
        axis=-1,
    )
    packed_grad = lax.optimization_barrier(packed_grad)
    r6 = grads((pick(attn_hidden), packed_grad), split=0)
    r6.go()
    norm_grad, gain_attn = norm_backward(
        dot_back(packed_grad, w_qkv), gains[1], attn_normed, attn_scale
    )
    gradient = gradient + norm_grad
    branch = (0.5 * gradient).astype(BF16)
    step(land=[r2], go=[r2], since=[packed_grad])
    branch = step(land=[r6], go=[r6], chain=branch)
    r7 = grads((pick_columns(plan, after_1, orders), branch), split=1)
    r7.go()
    before_grad = (dot_back(branch, w_ffn1_out) * swish_slope(before_1)).astype(BF16)
    before_grad = lax.optimization_barrier(before_grad)
    r8 = grads((pick(ffn1_hidden), before_grad), split=2)
    r8.go()
    step(land=[r1, r2, r3], go=[r1, r2, r3], since=[branch])
    step(land=[r7, r8], go=[r7, r8])
    before_grad = after(before_grad, jax.tree.leaves(ready(r1, r2, r3, r7, r8)))
    input_grad, gain_ffn1 = norm_backward(
        dot_back(before_grad, w_ffn1_in), gains[0], ffn1_normed, ffn1_scale
    )
    gradient = gradient + input_grad
    grad_gains = jnp.stack([gain_ffn1, gain_attn, gain_conv, gain_inner, gain_ffn2, gain_final])
    small_sums = jnp.concatenate([grad_gains, grad_kernel], axis=0)
    small_sums = jnp.dot(small_sums, tree_pick.astype(F32), precision=HIGHEST)
    r9 = Lane(small_grad_lane(plan, small_sums))
    finish(r1, r2, since=[before_grad])
    step(land=[r3], go=[r3], since=[before_grad])
    hold(r9, *r1.result, *r2.result)
    step(land=[r6], go=[r6])
    step(land=[r7], go=[r7], since=[input_grad, *waited(r6)])
    while r8.operand is not None:
        step(land=[r9], since=jax.tree.leaves(ready(r8)))
        r9.go()
        step(land=[r7, r8], go=[r7, r8])
        step(land=[r1, r2, r3, r6], go=[r1, r2, r3, r6], since=jax.tree.leaves(ready(r8))[:1])
    finish(r1, r2, r3, r6, r7, r9)
    (grad_ffn1_in,), (grad_ffn1_out,), (grad_qkv,) = r8.result, r7.result, r6.result
    grad_conv_out, grad_conv_in, grad_attn_out = r3.result
    (grad_ffn2_in,), (grad_ffn2_out,), small_shard = r2.result, r1.result, r9.result
    shard_gains, shard_kernel = small_shard[: grad_gains.shape[0]], small_shard[grad_gains.shape[0] :]

    return (
        layer_out,
        gradient.astype(BF16).reshape(inputs.shape),
        grad_ffn1_in,
        grad_ffn1_out,
        grad_qkv,
        grad_attn_out,
        grad_conv_in,
        shard_kernel,
        grad_conv_out,
        grad_ffn2_in,
        grad_ffn2_out,
        shard_gains,
    )


def solution(mesh):
    frames = P("rows", "wide", None)
    split_rows = P(BOTH, None)
    split_columns = P(None, BOTH)
    weights = (split_rows,) * 5 + (split_columns,) + (split_rows,) * 3 + (split_columns,)
    return jax.shard_map(
        per_device,
        mesh=mesh,
        in_specs=(frames, P("rows", None)) + weights + (frames,),
        out_specs=(frames, frames) + weights,
        check_vma=False,
    )
```

```python
import functools

import jax
import jax.numpy as jnp
import numpy as np
from jax import lax
from jax.experimental import pallas as pl
from jax.experimental.pallas import tpu as pltpu
from jax.sharding import PartitionSpec as P

HEADS = 16
HEAD_DIM = 64
EPSILON = 1e-05
BOTH = ("wide", "rows")
F32 = jnp.float32
BF16 = jnp.bfloat16
HIGHEST = lax.Precision.HIGHEST
VMEM_LIMIT = 60 * 1024 * 1024


class Plan:
    def __init__(self, wide, rows):
        self.wide, self.rows, self.total = wide, rows, wide * rows
        self.far = [k * 2 * rows for k in range(1, wide // 2)]
        row_bits = [1 << b for b in range(rows.bit_length() - 1)]
        self.flips = (row_bits, row_bits[1:] + row_bits[:1])
        self.stages = len(row_bits)
        self.far_bits = [1 << b for b in range((wide // 2).bit_length() - 1)]
        self.blocks = self.total // 2
        far = [0]
        for bit in reversed(self.far_bits):
            far += [k | bit for k in far]
        self.table = [
            np.array(
                [
                    (k * 2 * rows) ^ sum(f for t, f in enumerate(flips) if p >> t & 1)
                    for p in range(1 << self.stages)
                    for k in far
                ],
                np.int32,
            )
            for flips in self.flips
        ]

    def halvings(self):
        near = [self.stage_pairs(t) for t in reversed(range(self.stages))]
        return near + [self.flip_pairs(bit * 2 * self.rows) for bit in self.far_bits]

    def core_of(self, index):
        return (index // self.rows) % 2

    def stage_pairs(self, stage):
        return [(i, i ^ self.flips[self.core_of(i)][stage]) for i in range(self.total)]

    def flip_pairs(self, flip):
        return [(i, i ^ flip) for i in range(self.total)]

    def orders(self):
        index = lax.axis_index(BOTH)
        core = self.core_of(index)
        table = jnp.stack([jnp.asarray(t) for t in self.table])
        own = index ^ jnp.take(table, core, axis=0)
        other = (index ^ self.rows) ^ jnp.take(table, 1 - core, axis=0)
        return own, other


def send(x, pairs):
    return lax.ppermute(x, BOTH, pairs)


def held(arrays):
    return [pl.BlockSpec(memory_space=pl.ANY)] * len(arrays)


def there(tokens, before=None):
    tokens = jax.tree.leaves((tokens, before))
    if not tokens:
        return None

    def kernel(*refs):
        refs[-1][0] = 1

    return pl.pallas_call(
        kernel,
        out_shape=jax.ShapeDtypeStruct((1,), jnp.int32),
        in_specs=held(tokens),
        out_specs=pl.BlockSpec(memory_space=pltpu.SMEM),
        cost_estimate=pl.CostEstimate(flops=0, transcendentals=0, bytes_accessed=0),
        name="there",
    )(*tokens)


def after(values, tokens, before=None):
    flag = there(tokens, before) if jax.tree.leaves(tokens) else before
    if flag is None or not jax.tree.leaves(values):
        return values
    flag = flag[0] > 0
    return jax.tree.map(lambda x: jnp.where(flag, x, jnp.zeros((), x.dtype)), values)


class Lane:
    def __init__(self, steps):
        self.steps, self.result, self.arriving = steps, None, None
        self.operand, self.pairs = next(steps)

    def go(self):
        if isinstance(self.pairs[0], list):
            self.arriving = [send(x, pairs) for x, pairs in zip(self.operand, self.pairs)]
        else:
            self.arriving = jax.tree.map(lambda x: send(x, self.pairs), self.operand)

    def landed(self, arrived):
        self.arriving = None
        try:
            self.operand, self.pairs = self.steps.send(arrived)
        except StopIteration as stop:
            self.operand, self.result = None, stop.value


def step(land=(), go=(), chain=(), since=()):
    land = [lane for lane in land if lane.arriving is not None]
    flag = there(list(since)) if since else None
    for lane in land:
        lane.landed(after(lane.arriving, [], flag))
    if jax.tree.leaves(chain):
        chain = after(chain, jax.tree.leaves(ready(*land)))
    for lane in go:
        if lane.operand is not None and lane.arriving is None:
            lane.go()
    return chain


def hold(lane, *tokens):
    if lane.operand is not None:
        lane.operand = after(lane.operand, list(tokens))
        lane.go()


def waited(*lanes):
    return [lane.arriving for lane in lanes if lane.arriving is not None]


def ready(*lanes):
    return [lane.operand for lane in lanes if lane.operand is not None]


def finish(*lanes, since=()):
    while any(lane.operand is not None for lane in lanes):
        for lane in lanes:
            step(land=[lane], go=[lane], since=since)
    return lanes[0].result


def gather_lane(plan, shard, finish):
    held = shard[None]
    for bit in reversed(plan.far_bits):
        pairs = plan.flip_pairs(bit * 2 * plan.rows)
        arrived = yield held, pairs
        held = jnp.concatenate([held, arrived], axis=0)
    for stage in range(plan.stages - 1):
        held = jnp.concatenate([held, (yield held, plan.stage_pairs(stage))], axis=0)
    last = yield held, plan.stage_pairs(plan.stages - 1)
    from_core = yield [held, last], plan.flip_pairs(plan.rows)
    return finish([held, last, *from_core])


def grad_lane(plan, lefts, rights, split=0):
    others = [other for _, other in lefts]
    if len(rights) > 1:
        others, sent = [jnp.concatenate(others, axis=1)], [jnp.concatenate(rights, axis=1)]
    else:
        sent = rights
    arrived = yield [others[0], sent[0]], plan.flip_pairs(plan.rows)
    columns = np.cumsum([0] + [right.shape[1] for right in rights])
    size = lefts[0][0].shape[1]
    left = [
        jnp.concatenate([own, arrived[0][:, k * size : (k + 1) * size]], axis=0)
        for k, (own, _) in enumerate(lefts)
    ]
    both = [
        jnp.concatenate([right, arrived[1][:, columns[k] : columns[k + 1]]], axis=0)
        for k, right in enumerate(rights)
    ]
    left, both = lax.optimization_barrier((left, both))

    def products(first, last):
        parts = [
            dot_over_frames(one[:, size * first // 4 : size * last // 4], other).astype(BF16)
            for one, other in zip(left, both)
        ]
        return jnp.concatenate(parts, axis=1) if len(parts) > 1 else parts[0]

    away, kept = None, None
    halvings = plan.halvings()
    for count, pairs in enumerate(halvings):
        if count == 0:
            parts = (products(3, 4), products(2, 3)) if split else (products(2, 4),)
        elif count < split:
            half, quarter = kept.shape[0] // 2, kept.shape[0] // 4
            parts = (
                (kept[half + quarter :].astype(F32) + onward[quarter:].astype(F32)).astype(BF16),
                (kept[half : half + quarter].astype(F32) + onward[:quarter].astype(F32)).astype(BF16),
            )
        else:
            half = kept.shape[0] // 2
            parts = ((kept[half:].astype(F32) + onward.astype(F32)).astype(BF16),)
        if count == 0:
            kept = products(0, 2)
        else:
            kept = (kept[:half].astype(F32) + stay.astype(F32)).astype(BF16)
        if len(parts) == 2:
            onward, stay = yield list(parts), pairs
        else:
            arrived = yield parts[0], pairs
            onward, stay = arrived[arrived.shape[0] // 2 :], arrived[: arrived.shape[0] // 2]
    total = kept.astype(F32) + arrived.astype(F32)
    return [total[:, columns[k] : columns[k + 1]] for k in range(len(rights))]


def small_grad_lane(plan, both):
    half = both.shape[1] // 2
    total = both[:, :half] + (yield both[:, half:], plan.flip_pairs(plan.rows))
    for pairs in plan.halvings():
        half = total.shape[1] // 2
        total = total[:, :half] + (yield total[:, half:], pairs)
    return total


def heads_lane(plan, x):
    sent = x.reshape(plan.wide // 2, 2, *x.shape[1:])
    from_core = yield sent[:, 1], plan.flip_pairs(plan.rows)
    pair = jnp.stack([sent[:, 0], from_core], axis=1)
    arrived = yield (
        [pair[k] for k in range(1, plan.wide // 2)],
        [plan.flip_pairs(far) for far in plan.far],
    )
    return jnp.stack([pair[0], *arrived]).reshape(x.shape)


def assemble(plan, pieces, shapes, orders):
    half = plan.blocks // 2
    width = pieces[0].shape[-1]
    index = jnp.concatenate(orders)
    if any(rows % 16 for rows, _ in shapes):
        stacked = jnp.concatenate(pieces, axis=0)
        place = jnp.zeros((plan.total,), jnp.int32).at[index].set(jnp.arange(plan.total))
        stacked = jnp.take(stacked, place, axis=0)
        outs, start = [], 0
        for rows, columns in shapes:
            parts = []
            for _ in range(columns // width):
                parts.append(stacked[:, start : start + rows].reshape(-1, width))
                start += rows
            outs.append(jnp.concatenate(parts, axis=1))
        return outs

    def kernel(order, *refs):
        sources, outs = refs[:4], refs[4:-3]
        held, in_sems, out_sems = refs[-3:]
        loads = [
            pltpu.make_async_copy(sources[which], held.at[which], in_sems.at[which])
            for which in range(4)
        ]
        for load in loads:
            load.start()
        for which in range(4):
            loads[which].wait()
            for place in range(half):
                block = order[which * half + place]
                start = 0
                for out, (rows, columns) in enumerate(shapes):
                    for part in range(columns // width):
                        pltpu.make_async_copy(
                            held.at[which, place, pl.ds(start, rows)],
                            outs[out].at[
                                pl.ds(pl.multiple_of(block * rows, rows), rows),
                                pl.ds(part * width, width),
                            ],
                            out_sems.at[out],
                        ).start()
                        start += rows
        for out in range(len(shapes)):
            pltpu.make_async_copy(outs[out], outs[out], out_sems.at[out]).wait()

    return pl.pallas_call(
        kernel,
        out_shape=[
            jax.ShapeDtypeStruct((rows * plan.total, columns), BF16) for rows, columns in shapes
        ],
        in_specs=[pl.BlockSpec(memory_space=pltpu.SMEM)] + [pl.BlockSpec(memory_space=pl.ANY)] * 4,
        out_specs=[pl.BlockSpec(memory_space=pl.ANY)] * len(shapes),
        scratch_shapes=[
            pltpu.VMEM((4,) + pieces[0].shape, BF16),
            pltpu.SemaphoreType.DMA((4,)),
            pltpu.SemaphoreType.DMA((len(shapes),)),
        ],
        compiler_params=pltpu.CompilerParams(vmem_limit_bytes=24 * 1024 * 1024),
        cost_estimate=pl.CostEstimate(
            flops=0, transcendentals=0, bytes_accessed=8 * pieces[0].size * 2
        ),
        name="assemble",
    )(index, *pieces)


def pick_columns(plan, x, orders):
    index = jnp.concatenate(orders)
    length, columns = x.shape
    size = columns // plan.total
    if size % 128:
        split = jnp.take(x.reshape(length, plan.total, size), index, axis=1)
        split = split.reshape(length, columns)
        return split[:, : columns // 2], split[:, columns // 2 :]

    def kernel(order, source, first, second):
        for place in range(plan.total):
            out = (first, second)[place // plan.blocks]
            start = pl.multiple_of(order[place] * size, size)
            out[:, pl.ds((place % plan.blocks) * size, size)] = source[:, pl.ds(start, size)]

    whole = pl.BlockSpec(memory_space=pltpu.VMEM)
    return pl.pallas_call(
        kernel,
        out_shape=[jax.ShapeDtypeStruct((length, columns // 2), x.dtype)] * 2,
        in_specs=[pl.BlockSpec(memory_space=pltpu.SMEM), whole],
        out_specs=[whole] * 2,
        compiler_params=pltpu.CompilerParams(vmem_limit_bytes=16 * 1024 * 1024),
        cost_estimate=pl.CostEstimate(
            flops=0, transcendentals=0, bytes_accessed=4 * x.size
        ),
        name="pick_columns",
    )(index, x)


def dot(left, right):
    return jnp.dot(left, right, preferred_element_type=F32)


def dot_back(left, right):
    return lax.dot_general(left, right, (((1,), (1,)), ((), ())), preferred_element_type=F32)


def dot_over_frames(left, right):
    return lax.dot_general(left, right, (((0,), (0,)), ((), ())), preferred_element_type=F32)


def head_lanes(size, head):
    lane = lax.broadcasted_iota(jnp.int32, (1, size), 1)
    return (lane >= head * HEAD_DIM) & (lane < (head + 1) * HEAD_DIM)


def attend_kernel(q_ref, k_ref, v_ref, idq_ref, idk_ref, o_ref, total_ref):
    size = q_ref.shape[-1]
    query, keys, values = q_ref[0] * HEAD_DIM**-0.5, k_ref[0], v_ref[0]
    same = idq_ref[0] == idk_ref[0]
    mixed = jnp.zeros(query.shape, F32)
    totals = []
    for head in range(size // HEAD_DIM):
        lanes = head_lanes(size, head)
        scores = lax.dot_general(
            jnp.where(lanes, query, 0), keys, (((1,), (1,)), ((), ())), preferred_element_type=F32
        )
        scores = jnp.where(same, scores, -1e30)
        most = jnp.max(scores, axis=-1, keepdims=True)
        unnormed = jnp.exp(scores - most)
        total = jnp.sum(unnormed, axis=-1, keepdims=True)
        probs = (unnormed * (1.0 / total)).astype(BF16)
        mixed += jnp.dot(probs, jnp.where(lanes, values, 0), preferred_element_type=F32)
        totals.append(most + jnp.log(total))
    o_ref[0] = mixed.astype(BF16)
    total_ref[0] = jnp.concatenate(totals, axis=1)


def attend_back_kernel(
    q_ref, k_ref, v_ref, o_ref, do_ref, total_ref, idq_ref, idk_ref, cq_ref, sq_ref, ck_ref,
    sk_ref, turn_ref, dq_ref, dk_ref, dv_ref, dk_sum, dv_sum,
):
    step = pl.program_id(1)
    size = q_ref.shape[-1]
    scale = HEAD_DIM**-0.5
    query, keys, values, grads = q_ref[0] * scale, k_ref[0], v_ref[0], do_ref[0]
    different = idk_ref[0] != idq_ref[0]
    product = grads.astype(F32) * o_ref[0].astype(F32)

    @pl.when(step == 0)
    def _():
        dk_sum[...] = jnp.zeros_like(dk_sum)
        dv_sum[...] = jnp.zeros_like(dv_sum)

    turned_sum = jnp.zeros((size, query.shape[0]), F32)
    for head in range(size // HEAD_DIM):
        lanes = head_lanes(size, head)
        one_query = jnp.where(lanes, query, 0)
        one_grad = jnp.where(lanes, grads, 0)
        delta = lax.dot_general(
            jnp.where(lanes, jnp.ones((8, size), F32), 0.0),
            product,
            (((1,), (1,)), ((), ())),
            precision=HIGHEST,
            preferred_element_type=F32,
        )[:1]
        scores = lax.dot_general(
            keys, one_query, (((1,), (1,)), ((), ())), preferred_element_type=F32
        )
        probs = jnp.exp(jnp.where(different, -1e30, scores - total_ref[0, head : head + 1]))
        prob_grads = lax.dot_general(
            values, one_grad, (((1,), (1,)), ((), ())), preferred_element_type=F32
        )
        score_grads = (probs * (prob_grads - delta)).astype(BF16)
        dk_sum[...] += jnp.dot(score_grads, one_query, preferred_element_type=F32)
        dv_sum[...] += jnp.dot(probs.astype(BF16), one_grad, preferred_element_type=F32)
        turned_sum += dot_over_frames(jnp.where(lanes, keys, 0), score_grads)

    def turned(grad, cosine, sine):
        partner = jnp.dot(grad, turn_ref[...], precision=HIGHEST, preferred_element_type=F32)
        return (grad * cosine + partner * sine).astype(BF16)

    dq_ref[0] = turned(turned_sum.T * scale, cq_ref[0], sq_ref[0])

    @pl.when(step == pl.num_programs(1) - 1)
    def _():
        dk_ref[0] = turned(dk_sum[...], ck_ref[0], sk_ref[0])
        dv_ref[0] = dv_sum[...].astype(BF16)


def attend(query, keys, values, ids, tokens=()):
    rows, length, size = query.shape
    tile = 256
    heads = size // HEAD_DIM
    whole = pl.BlockSpec((1, length, size), lambda r, t: (r, 0, 0))
    part = pl.BlockSpec((1, tile, size), lambda r, t: (r, t, 0))
    return pl.pallas_call(
        lambda *refs: attend_kernel(*refs[:5], *refs[5 + len(tokens) :]),
        out_shape=[
            jax.ShapeDtypeStruct(query.shape, BF16),
            jax.ShapeDtypeStruct((rows, length, heads), F32),
        ],
        grid=(rows, length // tile),
        in_specs=[
            part,
            whole,
            whole,
            pl.BlockSpec((1, tile, 1), lambda r, t: (r, t, 0)),
            pl.BlockSpec((1, 1, length), lambda r, t: (r, 0, 0)),
            *held(tokens),
        ],
        out_specs=[part, pl.BlockSpec((1, tile, heads), lambda r, t: (r, t, 0))],
        compiler_params=pltpu.CompilerParams(vmem_limit_bytes=VMEM_LIMIT),
        name="attend",
    )(query, keys, values, ids[:, :, None], ids[:, None, :], *tokens)


def attend_back(query, keys, values, mixed, grads, totals, ids, cosine, sine, tokens=()):
    rows, length, size = query.shape
    tile = 1024 if length <= 1024 else 256
    heads = size // HEAD_DIM
    whole = pl.BlockSpec((1, length, size), lambda r, t: (r, 0, 0))
    part = pl.BlockSpec((1, tile, size), lambda r, t: (r, t, 0))
    lane = np.arange(size)
    turn = jnp.asarray((lane[:, None] == (lane ^ (HEAD_DIM // 2))[None, :]).astype(np.float32))
    return pl.pallas_call(
        lambda *refs: attend_back_kernel(*refs[:13], *refs[13 + len(tokens) :]),
        out_shape=[jax.ShapeDtypeStruct(query.shape, BF16)] * 3,
        grid=(rows, length // tile),
        in_specs=[
            part,
            whole,
            whole,
            part,
            part,
            pl.BlockSpec((1, heads, tile), lambda r, t: (r, 0, t)),
            pl.BlockSpec((1, 1, tile), lambda r, t: (r, 0, t)),
            pl.BlockSpec((1, length, 1), lambda r, t: (r, 0, 0)),
            part,
            part,
            whole,
            whole,
            pl.BlockSpec((size, size), lambda r, t: (0, 0)),
            *held(tokens),
        ],
        out_specs=[part, whole, whole],
        scratch_shapes=[pltpu.VMEM((length, size), F32)] * 2,
        compiler_params=pltpu.CompilerParams(vmem_limit_bytes=VMEM_LIMIT),
        name="attend_back",
    )(
        query, keys, values, mixed, grads, totals.transpose(0, 2, 1), ids[:, None, :],
        ids[:, :, None], cosine, sine, cosine, sine, turn, *tokens,
    )


def set_masks(ids_ref, ids, masks, count):
    ids[...] = jnp.broadcast_to(ids_ref[0], ids.shape)
    here = ids[pl.ds(masks.shape[0] // 2, count)]
    for tap in range(masks.shape[0]):
        masks[tap] = jnp.where(ids[pl.ds(tap, count)] == here, 1.0, 0.0)


def conv_kernel(ext_ref, ids_ref, taps_ref, out_ref, frames, ids, masks):
    count, taps = out_ref.shape[1], taps_ref.shape[0]

    @pl.when(pl.program_id(1) == 0)
    def _():
        set_masks(ids_ref, ids, masks, count)

    frames[...] = ext_ref[0].astype(F32)
    total = jnp.zeros((count, frames.shape[1]), F32)
    for odd in range(8):
        shifted = frames[pl.ds(odd, frames.shape[0] - 8)]
        for tap in range(odd, taps, 8):
            part = shifted[tap - odd : tap - odd + count]
            total += part * masks[tap] * taps_ref[tap : tap + 1]
    out_ref[0] = total


def conv_back_kernel(
    ext_ref, ids_ref, grad_ref, taps_ref, dtaps_ref, dext_ref, frames, ids, masks, total, some
):
    count, taps = grad_ref.shape[1], taps_ref.shape[0]

    @pl.when(pl.program_id(1) == 0)
    def _():
        set_masks(ids_ref, ids, masks, count)

    frames[...] = ext_ref[0].astype(F32)
    grad = grad_ref[0]
    total[...] = jnp.zeros_like(total)
    rows = [None] * taps
    for odd in range(8):
        shifted = frames[pl.ds(odd, frames.shape[0] - 8)]
        some[...] = jnp.zeros_like(some)
        for tap in range(odd, taps, 8):
            kept = grad * masks[tap]
            rows[tap] = jnp.sum(shifted[tap - odd : tap - odd + count] * kept, axis=0, keepdims=True)
            some[pl.ds(tap - odd, count)] += kept * taps_ref[tap : tap + 1]
        total[pl.ds(odd, some.shape[0])] += some[...]
    dext_ref[0] = total[...]
    dtaps_ref[0] = jnp.concatenate(rows, axis=0)


def depthwise(extended, ids, taps, tokens=()):
    rows, padded, width = extended.shape
    count = padded - 32
    block = 128
    return pl.pallas_call(
        lambda *refs: conv_kernel(*refs[:3], *refs[3 + len(tokens) :]),
        out_shape=jax.ShapeDtypeStruct((rows, count, width), F32),
        grid=(rows, width // block),
        in_specs=[
            pl.BlockSpec((1, padded, block), lambda r, c: (r, 0, c)),
            pl.BlockSpec((1, padded, 1), lambda r, c: (r, 0, 0)),
            pl.BlockSpec((taps.shape[0], block), lambda r, c: (0, c)),
            *held(tokens),
        ],
        out_specs=pl.BlockSpec((1, count, block), lambda r, c: (r, 0, c)),
        scratch_shapes=[pltpu.VMEM((padded, block), F32)] * 2
        + [pltpu.VMEM((taps.shape[0], count, block), F32)],
        compiler_params=pltpu.CompilerParams(vmem_limit_bytes=16 * 1024 * 1024),
        name="depthwise",
    )(extended, ids, taps, *tokens)


def depthwise_back(extended, ids, grad, taps, tokens=()):
    rows, padded, width = extended.shape
    count = padded - 32
    block = 128
    return pl.pallas_call(
        lambda *refs: conv_back_kernel(*refs[:4], *refs[4 + len(tokens) :]),
        out_shape=[
            jax.ShapeDtypeStruct((rows, taps.shape[0], width), F32),
            jax.ShapeDtypeStruct((rows, padded, width), F32),
        ],
        grid=(rows, width // block),
        in_specs=[
            pl.BlockSpec((1, padded, block), lambda r, c: (r, 0, c)),
            pl.BlockSpec((1, padded, 1), lambda r, c: (r, 0, 0)),
            pl.BlockSpec((1, count, block), lambda r, c: (r, 0, c)),
            pl.BlockSpec((taps.shape[0], block), lambda r, c: (0, c)),
            *held(tokens),
        ],
        out_specs=[
            pl.BlockSpec((1, taps.shape[0], block), lambda r, c: (r, 0, c)),
            pl.BlockSpec((1, padded, block), lambda r, c: (r, 0, c)),
        ],
        scratch_shapes=[pltpu.VMEM((padded, block), F32)] * 2
        + [
            pltpu.VMEM((taps.shape[0], count, block), F32),
            pltpu.VMEM((padded, block), F32),
            pltpu.VMEM((padded - 8, block), F32),
        ],
        compiler_params=pltpu.CompilerParams(vmem_limit_bytes=16 * 1024 * 1024),
        name="depthwise_back",
    )(extended, ids, grad, taps, *tokens)


def segment_info(lengths, frame_total):
    segment_end = jnp.cumsum(lengths, axis=-1, dtype=jnp.int32)
    frame_index = jnp.arange(frame_total, dtype=jnp.int32)
    passed = (frame_index[None, None, :] >= segment_end[:, :, None]).astype(jnp.int32)
    segment_ids = jnp.sum(passed, axis=1, dtype=jnp.int32)
    seg_starts = jnp.sum(passed * lengths[:, :, None], axis=1, dtype=jnp.int32)
    return (segment_ids, frame_index[None, :] - seg_starts)


def layer_norm(values, gain_row):
    centred = values - jnp.mean(values, axis=-1, keepdims=True)
    inv_scale = lax.rsqrt(jnp.mean(centred * centred, axis=-1, keepdims=True) + EPSILON)
    normed = centred * inv_scale
    return (normed * gain_row, normed, inv_scale)


def norm_backward(gradient, gain_row, normed, inv_scale):
    scaled = gradient * gain_row
    gain_grad = jnp.sum(gradient * normed, axis=0)
    centred_mean = jnp.mean(scaled, axis=-1, keepdims=True)
    product_mean = jnp.mean(scaled * normed, axis=-1, keepdims=True)
    return (inv_scale * (scaled - centred_mean - normed * product_mean), gain_grad)


def swish_slope(values):
    gate_sig = jax.nn.sigmoid(values)
    return gate_sig * (1.0 + values * (1.0 - gate_sig))


def neighbours(x, width, axis):
    size, length = lax.axis_size("wide"), x.shape[axis]
    up = [(i, i + 1) for i in range(size - 1)]
    before = lax.ppermute(lax.slice_in_dim(x, length - width, length, axis=axis), "wide", up)
    after = lax.ppermute(
        lax.slice_in_dim(x, 0, width, axis=axis), "wide", [(j, i) for i, j in up]
    )
    return before, after


def half_turn(values):
    half = HEAD_DIM // 2
    lane = lax.broadcasted_iota(jnp.int32, (1, values.shape[-1]), 1) % HEAD_DIM
    ahead = jnp.roll(values, -half, axis=-1)
    behind = jnp.roll(values, half, axis=-1)
    return jnp.where(lane < half, -ahead, behind)


def per_device(
    inputs,
    lengths,
    ffn1_in,
    ffn1_out,
    attn_qkv,
    attn_out,
    conv_in,
    depth_kernel,
    conv_out,
    ffn2_in,
    ffn2_out,
    norm_gains,
    cotangent,
):
    wide, rows = lax.axis_size("wide"), lax.axis_size("rows")
    plan = Plan(wide, rows)
    row_count, frames_here, width = inputs.shape
    tokens = row_count * frames_here
    frame_total = frames_here * wide
    taps = depth_kernel.shape[0]
    half_width = taps // 2
    me = lax.axis_index("wide")
    orders = plan.orders()
    segment_ids, position = segment_info(lengths, frame_total)

    def packed_shards(shards):
        parts = []
        for shard in shards:
            for column in range(0, shard.shape[1], width):
                parts.append(shard[:, column : column + width])
        return jnp.concatenate(parts, axis=0) if len(parts) > 1 else parts[0]

    def weights_lane(*shards):
        shapes = [shard.shape for shard in shards]
        return Lane(
            gather_lane(
                plan, packed_shards(shards), lambda held: assemble(plan, held, shapes, orders)
            )
        )

    def small_lane(small):
        flip = 1
        while flip < plan.total:
            small = jnp.concatenate([small, (yield small, plan.flip_pairs(flip))], axis=1)
            flip *= 2
        return dot_back(small, small_pick.astype(BF16))

    feature = jnp.arange(width, dtype=jnp.int32)
    block = width // plan.total
    small_source = (feature // block ^ lax.axis_index(BOTH)) * block + feature % block
    small_pick = feature[:, None] == small_source[None, :]
    small = Lane(small_lane(jnp.concatenate([norm_gains, depth_kernel], axis=0)))
    g1, g2 = weights_lane(ffn1_in), weights_lane(ffn1_out)
    w_qkv = lax.all_gather(attn_qkv, BOTH, axis=0, tiled=True)
    wides = (attn_out, conv_in, conv_out)
    middle = lax.all_gather(jnp.concatenate(wides, axis=1), BOTH, axis=0, tiled=True)
    cuts = np.cumsum([0] + [shard.shape[1] for shard in wides])
    w_attn_out, w_conv_in, w_conv_out = (
        middle[:, start:stop] for start, stop in zip(cuts[:-1], cuts[1:])
    )
    w_ffn2_in = lax.all_gather(ffn2_in, BOTH, axis=0, tiled=True)
    g4 = weights_lane(ffn2_out)

    source = jnp.repeat(jnp.concatenate(orders), block) * block + feature % block
    tree_pick = (feature[:, None] == source[None, :]).astype(BF16)
    group = width // wide
    head_source = (feature // group ^ me) * group + feature % group
    head_pick = (feature[:, None] == head_source[None, :]).astype(BF16)

    def pick(x):
        both = dot(x, tree_pick).astype(BF16)
        return both[:, : width // 2], both[:, width // 2 :]

    def to_groups(x):
        return dot(x, head_pick).astype(BF16).reshape(tokens, wide, group).transpose(1, 0, 2)

    def from_groups(x):
        return dot_back(x.transpose(1, 0, 2).reshape(tokens, width), head_pick).astype(BF16)

    offset = me * frames_here
    padded_ids = jnp.pad(segment_ids, ((0, 0), (half_width, 32 - half_width)), constant_values=-1)
    edge_ids = lax.dynamic_slice_in_dim(padded_ids, offset, frames_here + 32, 1)
    edge_ids = edge_ids.astype(F32)[:, :, None]
    local_position = lax.dynamic_slice_in_dim(position, offset, frames_here, 1)
    by_device = jnp.arange(wide, dtype=jnp.int32) ^ me

    def row_order(x):
        x = x.reshape(row_count, wide, frames_here)
        return jnp.take(x, by_device, axis=1).reshape(row_count, frame_total)

    row_ids, row_position = row_order(segment_ids), row_order(position)

    def rotation(at, size):
        lane = jnp.arange(size, dtype=jnp.int32) % HEAD_DIM
        frequency = jnp.power(
            10000.0, -2.0 * (lane % (HEAD_DIM // 2)).astype(F32) / HEAD_DIM
        )
        angles = at.astype(F32)[..., None] * frequency
        sign = jnp.where(lane < HEAD_DIM // 2, 1.0, -1.0)
        return jnp.cos(angles), jnp.sin(angles), sign

    cosine, sine, _ = rotation(local_position.reshape(tokens), HEAD_DIM)
    cosine = jnp.tile(cosine, (1, HEADS))
    sine = jnp.tile(sine, (1, HEADS))
    row_cosine, row_sine, sign = rotation(row_position, group)
    row_sine = row_sine * sign

    tables = (row_cosine, row_sine, cosine, sine, edge_ids)
    def follow(lane, leader):
        lane.operand = after(lane.operand, jax.tree.leaves(ready(leader)))
        lane.go()

    step(go=[g1, small])
    for _ in range(3):
        step(land=[small], go=[small])
    step(land=[g1, small], go=[small])
    follow(g1, small)
    finish(small)
    gains, kernel = small.result[: norm_gains.shape[0]], small.result[norm_gains.shape[0] :]
    residual = inputs.astype(F32).reshape(tokens, width)
    ffn1_norm, ffn1_normed, ffn1_scale = layer_norm(residual, gains[0])
    ffn1_hidden = after(ffn1_norm.astype(BF16), tables)
    follow(g2, g1)
    step(land=[g1])
    g1.operand = after(g1.operand, [gains])
    g1.go()
    step(land=[g2])
    follow(g2, g1)
    for _ in range(2):
        step(land=[g1], go=[g1])
        step(land=[g2])
        follow(g2, g1)
    follow(g4, g2)
    (w_ffn1_in,) = finish(g1)
    before_1 = dot(ffn1_hidden, w_ffn1_in)
    after_1 = (before_1 * jax.nn.sigmoid(before_1)).astype(BF16)
    (w_ffn1_out,) = finish(g2)
    first = residual + 0.5 * dot(after_1, w_ffn1_out)
    attn_norm, attn_normed, attn_scale = layer_norm(first, gains[1])
    attn_hidden = attn_norm.astype(BF16)
    packed = dot(attn_hidden, w_qkv)
    step(land=[g4], go=[g4], since=[packed])
    queries = packed[:, :width]
    keys = packed[:, width : 2 * width]
    queries = (queries * cosine + half_turn(queries) * sine).astype(BF16)
    keys = (keys * cosine + half_turn(keys) * sine).astype(BF16)
    values = packed[:, 2 * width :].astype(BF16)
    heads = Lane(
        heads_lane(
            plan,
            jnp.concatenate([to_groups(queries), to_groups(keys), to_groups(values)], axis=-1),
        )
    )

    def as_rows(x):
        x = x.reshape(wide, row_count, frames_here, group)
        return x.transpose(1, 0, 2, 3).reshape(row_count, frame_total, group)

    def as_blocks(x):
        x = x.reshape(row_count, wide, frames_here, group)
        return x.transpose(1, 0, 2, 3).reshape(wide, tokens, group)

    step(go=[heads])
    step(land=[heads], go=[heads])
    step(land=[g4], since=ready(heads)[0])
    arrived = finish(heads)
    hold(g4, arrived)
    row_queries = as_rows(arrived[..., :group])
    row_keys = as_rows(arrived[..., group : 2 * group])
    row_values = as_rows(arrived[..., 2 * group :])
    mixed_rows, row_totals = attend(row_queries, row_keys, row_values, row_ids)
    heads = Lane(heads_lane(plan, as_blocks(mixed_rows)))
    step(go=[heads])
    step(land=[heads], go=[heads])
    step(land=[g4], go=[g4], since=ready(heads)[0])
    mixed = from_groups(finish(heads))
    second = first + dot(mixed, w_attn_out)
    conv_norm, conv_normed, conv_scale = layer_norm(second, gains[2])
    conv_hidden = conv_norm.astype(BF16)
    gated = dot(conv_hidden, w_conv_in)
    gate_sig = jax.nn.sigmoid(gated[:, width:])
    glu = (gated[:, :width] * gate_sig).astype(BF16).reshape(row_count, frames_here, width)
    before, after_frames = neighbours(glu, half_width, 1)
    extended = jnp.concatenate(
        [before, glu, after_frames, jnp.zeros((row_count, 32 - 2 * half_width, width), BF16)],
        axis=1,
    )
    step(land=[g4], go=[g4], since=[gate_sig])
    convolved = depthwise(extended, edge_ids, kernel).reshape(tokens, width)
    inner_out, inner_normed, inner_scale = layer_norm(convolved, gains[3])
    activated = (inner_out * jax.nn.sigmoid(inner_out)).astype(BF16)
    third = second + dot(activated, w_conv_out)
    ffn2_norm, ffn2_normed, ffn2_scale = layer_norm(third, gains[4])
    ffn2_hidden = ffn2_norm.astype(BF16)
    before_2 = dot(ffn2_hidden, w_ffn2_in)
    after_2 = (before_2 * jax.nn.sigmoid(before_2)).astype(BF16)
    (w_ffn2_out,) = finish(g4)
    fourth = third + 0.5 * dot(after_2, w_ffn2_out)
    final_out, final_normed, final_scale = layer_norm(fourth, gains[5])
    layer_out = final_out.astype(BF16).reshape(inputs.shape)

    def grads(*pairs, split=0):
        lefts, rights = [left for left, _ in pairs], [right for _, right in pairs]
        return Lane(grad_lane(plan, lefts, rights, split))

    gradient, gain_final = norm_backward(
        cotangent.astype(F32).reshape(tokens, width), gains[5], final_normed, final_scale
    )
    branch = (0.5 * gradient).astype(BF16)
    r1 = grads((pick_columns(plan, after_2, orders), branch))
    r1.go()
    before_grad = (dot_back(branch, w_ffn2_out) * swish_slope(before_2)).astype(BF16)
    r2 = grads((pick(ffn2_hidden), before_grad))
    r2.go()
    step(land=[r1], go=[r1])
    input_grad, gain_ffn2 = norm_backward(
        dot_back(before_grad, w_ffn2_in), gains[4], ffn2_normed, ffn2_scale
    )
    gradient = gradient + input_grad
    conv_branch = after(gradient.astype(BF16), jax.tree.leaves(ready(r1)))
    act_grad = dot_back(conv_branch, w_conv_out) * swish_slope(inner_out)
    conv_grad, gain_inner = norm_backward(act_grad, gains[3], inner_normed, inner_scale)
    step(land=[r2], go=[r2])
    kernel_terms, ext_grad = depthwise_back(
        extended,
        edge_ids,
        conv_grad.reshape(row_count, frames_here, width),
        kernel,
        jax.tree.leaves(ready(r1, r2)),
    )
    grad_kernel = jnp.sum(kernel_terms, axis=0)
    end = half_width + frames_here
    rims = ext_grad[:, :half_width], ext_grad[:, end : end + half_width]
    to_before, to_after = (rim.astype(BF16) for rim in rims)
    up = [(i, i + 1) for i in range(wide - 1)]
    from_before = lax.ppermute(to_after, "wide", up).astype(F32)
    from_after = lax.ppermute(to_before, "wide", [(j, i) for i, j in up]).astype(F32)
    middle = jnp.zeros((row_count, frames_here - 2 * half_width, width), F32)
    glu_grad = ext_grad[:, half_width:end] + jnp.concatenate(
        [from_before, middle, from_after], axis=1
    )
    glu_grad = glu_grad.reshape(tokens, width)
    gated_grad = jnp.concatenate(
        [glu_grad * gate_sig, glu_grad * gated[:, :width] * gate_sig * (1.0 - gate_sig)],
        axis=-1,
    ).astype(BF16)
    norm_grad, gain_conv = norm_backward(
        dot_back(gated_grad, w_conv_in), gains[2], conv_normed, conv_scale
    )
    gradient = gradient + norm_grad
    attn_branch = gradient.astype(BF16)
    head_grads = dot_back(attn_branch, w_attn_out).astype(BF16)
    heads = Lane(heads_lane(plan, to_groups(head_grads)))
    r3 = grads(
        (pick(activated), conv_branch), (pick(conv_hidden), gated_grad), (pick(mixed), attn_branch)
    )
    step(go=[heads, r3])
    step(land=[heads], go=[heads])
    step(land=[r1, r3], go=[r1, r3], since=ready(heads)[0])
    row_grads = as_rows(finish(heads))
    query_grad, key_grad, value_grad = attend_back(
        row_queries,
        row_keys,
        row_values,
        mixed_rows,
        row_grads,
        row_totals,
        row_ids,
        row_cosine,
        row_sine,
        jax.tree.leaves(ready(r1, r3)),
    )
    heads = Lane(
        heads_lane(
            plan,
            jnp.concatenate(
                [as_blocks(query_grad), as_blocks(key_grad), as_blocks(value_grad)], axis=-1
            ),
        )
    )
    step(go=[heads])
    step(land=[heads], go=[heads])
    step(land=[r1, r2, r3], go=[r2, r3], since=ready(heads)[0])
    returned = finish(heads)
    returned = after(returned, jax.tree.leaves(ready(r1, r2, r3)))
    hold(r1, returned)
    packed_grad = jnp.concatenate(
        [from_groups(returned[..., part * group : (part + 1) * group]) for part in range(3)],
        axis=-1,
    )
    packed_grad = lax.optimization_barrier(packed_grad)
    r6 = grads((pick(attn_hidden), packed_grad), split=0)
    r6.go()
    norm_grad, gain_attn = norm_backward(
        dot_back(packed_grad, w_qkv), gains[1], attn_normed, attn_scale
    )
    gradient = gradient + norm_grad
    branch = (0.5 * gradient).astype(BF16)
    step(land=[r2], go=[r2], since=[packed_grad])
    branch = step(land=[r6], go=[r6], chain=branch)
    r7 = grads((pick_columns(plan, after_1, orders), branch), split=1)
    r7.go()
    before_grad = (dot_back(branch, w_ffn1_out) * swish_slope(before_1)).astype(BF16)
    before_grad = lax.optimization_barrier(before_grad)
    r8 = grads((pick(ffn1_hidden), before_grad), split=2)
    r8.go()
    step(land=[r1, r2, r3], go=[r1, r2, r3], since=[branch])
    step(land=[r7, r8], go=[r7, r8])
    before_grad = after(before_grad, jax.tree.leaves(ready(r1, r2, r3, r7, r8)))
    input_grad, gain_ffn1 = norm_backward(
        dot_back(before_grad, w_ffn1_in), gains[0], ffn1_normed, ffn1_scale
    )
    gradient = gradient + input_grad
    grad_gains = jnp.stack([gain_ffn1, gain_attn, gain_conv, gain_inner, gain_ffn2, gain_final])
    small_sums = jnp.concatenate([grad_gains, grad_kernel], axis=0)
    small_sums = jnp.dot(small_sums, tree_pick.astype(F32), precision=HIGHEST)
    r9 = Lane(small_grad_lane(plan, small_sums))
    finish(r1, r2, since=[before_grad])
    step(land=[r3], go=[r3], since=[before_grad])
    hold(r9, *r1.result, *r2.result)
    step(land=[r6], go=[r6])
    step(land=[r7], go=[r7], since=[input_grad, *waited(r6)])
    while r8.operand is not None:
        step(land=[r9], since=jax.tree.leaves(ready(r8)))
        r9.go()
        step(land=[r7, r8], go=[r7, r8])
        step(land=[r1, r2, r3, r6], go=[r1, r2, r3, r6], since=jax.tree.leaves(ready(r8))[:1])
    finish(r1, r2, r3, r6, r7, r9)
    (grad_ffn1_in,), (grad_ffn1_out,), (grad_qkv,) = r8.result, r7.result, r6.result
    grad_conv_out, grad_conv_in, grad_attn_out = r3.result
    (grad_ffn2_in,), (grad_ffn2_out,), small_shard = r2.result, r1.result, r9.result
    shard_gains, shard_kernel = small_shard[: grad_gains.shape[0]], small_shard[grad_gains.shape[0] :]

    return (
        layer_out,
        gradient.astype(BF16).reshape(inputs.shape),
        grad_ffn1_in,
        grad_ffn1_out,
        grad_qkv,
        grad_attn_out,
        grad_conv_in,
        shard_kernel,
        grad_conv_out,
        grad_ffn2_in,
        grad_ffn2_out,
        shard_gains,
    )


def solution(mesh):
    frames = P("rows", "wide", None)
    split_rows = P(BOTH, None)
    split_columns = P(None, BOTH)
    weights = (split_rows,) * 5 + (split_columns,) + (split_rows,) * 3 + (split_columns,)
    return jax.shard_map(
        per_device,
        mesh=mesh,
        in_specs=(frames, P("rows", None)) + weights + (frames,),
        out_specs=(frames, frames) + weights,
        check_vma=False,
    )
```

```python
import functools

import jax
import jax.numpy as jnp
import numpy as np
from jax import lax
from jax.experimental import pallas as pl
from jax.experimental.pallas import tpu as pltpu
from jax.sharding import PartitionSpec as P

HEADS = 16
HEAD_DIM = 64
EPSILON = 1e-05
BOTH = ("wide", "rows")
F32 = jnp.float32
BF16 = jnp.bfloat16
HIGHEST = lax.Precision.HIGHEST
VMEM_LIMIT = 60 * 1024 * 1024


class Plan:
    def __init__(self, wide, rows):
        self.wide, self.rows, self.total = wide, rows, wide * rows
        self.far = [k * 2 * rows for k in range(1, wide // 2)]
        row_bits = [1 << b for b in range(rows.bit_length() - 1)]
        self.flips = (row_bits, row_bits[1:] + row_bits[:1])
        self.stages = len(row_bits)
        self.far_bits = [1 << b for b in range((wide // 2).bit_length() - 1)]
        self.blocks = self.total // 2
        far = [0]
        for bit in reversed(self.far_bits):
            far += [k | bit for k in far]
        self.table = [
            np.array(
                [
                    (k * 2 * rows) ^ sum(f for t, f in enumerate(flips) if p >> t & 1)
                    for p in range(1 << self.stages)
                    for k in far
                ],
                np.int32,
            )
            for flips in self.flips
        ]

    def halvings(self):
        near = [self.stage_pairs(t) for t in reversed(range(self.stages))]
        return near + [self.flip_pairs(bit * 2 * self.rows) for bit in self.far_bits]

    def core_of(self, index):
        return (index // self.rows) % 2

    def stage_pairs(self, stage):
        return [(i, i ^ self.flips[self.core_of(i)][stage]) for i in range(self.total)]

    def flip_pairs(self, flip):
        return [(i, i ^ flip) for i in range(self.total)]

    def orders(self):
        index = lax.axis_index(BOTH)
        core = self.core_of(index)
        table = jnp.stack([jnp.asarray(t) for t in self.table])
        own = index ^ jnp.take(table, core, axis=0)
        other = (index ^ self.rows) ^ jnp.take(table, 1 - core, axis=0)
        return own, other


def send(x, pairs):
    return lax.ppermute(x, BOTH, pairs)


def held(arrays):
    return [pl.BlockSpec(memory_space=pl.ANY)] * len(arrays)


def there(tokens, before=None):
    tokens = jax.tree.leaves((tokens, before))
    if not tokens:
        return None

    def kernel(*refs):
        refs[-1][0] = 1

    return pl.pallas_call(
        kernel,
        out_shape=jax.ShapeDtypeStruct((1,), jnp.int32),
        in_specs=held(tokens),
        out_specs=pl.BlockSpec(memory_space=pltpu.SMEM),
        cost_estimate=pl.CostEstimate(flops=0, transcendentals=0, bytes_accessed=0),
        name="there",
    )(*tokens)


def after(values, tokens, before=None):
    flag = there(tokens, before) if jax.tree.leaves(tokens) else before
    if flag is None or not jax.tree.leaves(values):
        return values
    flag = flag[0] > 0
    return jax.tree.map(lambda x: jnp.where(flag, x, jnp.zeros((), x.dtype)), values)


class Lane:
    def __init__(self, steps):
        self.steps, self.result, self.arriving = steps, None, None
        self.operand, self.pairs = next(steps)

    def go(self):
        if isinstance(self.pairs[0], list):
            self.arriving = [send(x, pairs) for x, pairs in zip(self.operand, self.pairs)]
        else:
            self.arriving = jax.tree.map(lambda x: send(x, self.pairs), self.operand)

    def landed(self, arrived):
        self.arriving = None
        try:
            self.operand, self.pairs = self.steps.send(arrived)
        except StopIteration as stop:
            self.operand, self.result = None, stop.value


def step(land=(), go=(), chain=(), since=()):
    land = [lane for lane in land if lane.arriving is not None]
    flag = there(list(since)) if since else None
    for lane in land:
        lane.landed(after(lane.arriving, [], flag))
    if jax.tree.leaves(chain):
        chain = after(chain, jax.tree.leaves(ready(*land)))
    for lane in go:
        if lane.operand is not None and lane.arriving is None:
            lane.go()
    return chain


def hold(lane, *tokens):
    if lane.operand is not None:
        lane.operand = after(lane.operand, list(tokens))
        lane.go()


def waited(*lanes):
    return [lane.arriving for lane in lanes if lane.arriving is not None]


def ready(*lanes):
    return [lane.operand for lane in lanes if lane.operand is not None]


def finish(*lanes, since=()):
    while any(lane.operand is not None for lane in lanes):
        for lane in lanes:
            step(land=[lane], go=[lane], since=since)
    return lanes[0].result


def gather_lane(plan, shard, finish):
    held = shard[None]
    for bit in reversed(plan.far_bits):
        pairs = plan.flip_pairs(bit * 2 * plan.rows)
        arrived = yield held, pairs
        held = jnp.concatenate([held, arrived], axis=0)
    for stage in range(plan.stages - 1):
        held = jnp.concatenate([held, (yield held, plan.stage_pairs(stage))], axis=0)
    last = yield held, plan.stage_pairs(plan.stages - 1)
    from_core = yield [held, last], plan.flip_pairs(plan.rows)
    return finish([held, last, *from_core])


def grad_lane(plan, lefts, rights, split=0):
    others = [other for _, other in lefts]
    if len(rights) > 1:
        others, sent = [jnp.concatenate(others, axis=1)], [jnp.concatenate(rights, axis=1)]
    else:
        sent = rights
    arrived = yield [others[0], sent[0]], plan.flip_pairs(plan.rows)
    columns = np.cumsum([0] + [right.shape[1] for right in rights])
    size = lefts[0][0].shape[1]
    left = [
        jnp.concatenate([own, arrived[0][:, k * size : (k + 1) * size]], axis=0)
        for k, (own, _) in enumerate(lefts)
    ]
    both = [
        jnp.concatenate([right, arrived[1][:, columns[k] : columns[k + 1]]], axis=0)
        for k, right in enumerate(rights)
    ]
    left, both = lax.optimization_barrier((left, both))

    def products(first, last):
        parts = [
            dot_over_frames(one[:, size * first // 4 : size * last // 4], other).astype(BF16)
            for one, other in zip(left, both)
        ]
        return jnp.concatenate(parts, axis=1) if len(parts) > 1 else parts[0]

    away, kept = None, None
    halvings = plan.halvings()
    for count, pairs in enumerate(halvings):
        if count == 0:
            parts = (products(3, 4), products(2, 3)) if split else (products(2, 4),)
        elif count < split:
            half, quarter = kept.shape[0] // 2, kept.shape[0] // 4
            parts = (
                (kept[half + quarter :].astype(F32) + onward[quarter:].astype(F32)).astype(BF16),
                (kept[half : half + quarter].astype(F32) + onward[:quarter].astype(F32)).astype(BF16),
            )
        else:
            half = kept.shape[0] // 2
            parts = ((kept[half:].astype(F32) + onward.astype(F32)).astype(BF16),)
        if count == 0:
            kept = products(0, 2)
        else:
            kept = (kept[:half].astype(F32) + stay.astype(F32)).astype(BF16)
        if len(parts) == 2:
            onward, stay = yield list(parts), pairs
        else:
            arrived = yield parts[0], pairs
            onward, stay = arrived[arrived.shape[0] // 2 :], arrived[: arrived.shape[0] // 2]
    total = kept.astype(F32) + arrived.astype(F32)
    return [total[:, columns[k] : columns[k + 1]] for k in range(len(rights))]


def small_grad_lane(plan, both):
    half = both.shape[1] // 2
    total = both[:, :half] + (yield both[:, half:], plan.flip_pairs(plan.rows))
    for pairs in plan.halvings():
        half = total.shape[1] // 2
        total = total[:, :half] + (yield total[:, half:], pairs)
    return total


def heads_lane(plan, x):
    sent = x.reshape(plan.wide // 2, 2, *x.shape[1:])
    from_core = yield sent[:, 1], plan.flip_pairs(plan.rows)
    pair = jnp.stack([sent[:, 0], from_core], axis=1)
    arrived = yield (
        [pair[k] for k in range(1, plan.wide // 2)],
        [plan.flip_pairs(far) for far in plan.far],
    )
    return jnp.stack([pair[0], *arrived]).reshape(x.shape)


def assemble(plan, pieces, shapes, orders):
    half = plan.blocks // 2
    width = pieces[0].shape[-1]
    index = jnp.concatenate(orders)
    if any(rows % 16 for rows, _ in shapes):
        stacked = jnp.concatenate(pieces, axis=0)
        place = jnp.zeros((plan.total,), jnp.int32).at[index].set(jnp.arange(plan.total))
        stacked = jnp.take(stacked, place, axis=0)
        outs, start = [], 0
        for rows, columns in shapes:
            parts = []
            for _ in range(columns // width):
                parts.append(stacked[:, start : start + rows].reshape(-1, width))
                start += rows
            outs.append(jnp.concatenate(parts, axis=1))
        return outs

    def kernel(order, *refs):
        sources, outs = refs[:4], refs[4:-3]
        held, in_sems, out_sems = refs[-3:]
        loads = [
            pltpu.make_async_copy(sources[which], held.at[which], in_sems.at[which])
            for which in range(4)
        ]
        for load in loads:
            load.start()
        for which in range(4):
            loads[which].wait()
            for place in range(half):
                block = order[which * half + place]
                start = 0
                for out, (rows, columns) in enumerate(shapes):
                    for part in range(columns // width):
                        pltpu.make_async_copy(
                            held.at[which, place, pl.ds(start, rows)],
                            outs[out].at[
                                pl.ds(pl.multiple_of(block * rows, rows), rows),
                                pl.ds(part * width, width),
                            ],
                            out_sems.at[out],
                        ).start()
                        start += rows
        for out in range(len(shapes)):
            pltpu.make_async_copy(outs[out], outs[out], out_sems.at[out]).wait()

    return pl.pallas_call(
        kernel,
        out_shape=[
            jax.ShapeDtypeStruct((rows * plan.total, columns), BF16) for rows, columns in shapes
        ],
        in_specs=[pl.BlockSpec(memory_space=pltpu.SMEM)] + [pl.BlockSpec(memory_space=pl.ANY)] * 4,
        out_specs=[pl.BlockSpec(memory_space=pl.ANY)] * len(shapes),
        scratch_shapes=[
            pltpu.VMEM((4,) + pieces[0].shape, BF16),
            pltpu.SemaphoreType.DMA((4,)),
            pltpu.SemaphoreType.DMA((len(shapes),)),
        ],
        compiler_params=pltpu.CompilerParams(vmem_limit_bytes=24 * 1024 * 1024),
        cost_estimate=pl.CostEstimate(
            flops=0, transcendentals=0, bytes_accessed=8 * pieces[0].size * 2
        ),
        name="assemble",
    )(index, *pieces)


def pick_columns(plan, x, orders):
    index = jnp.concatenate(orders)
    length, columns = x.shape
    size = columns // plan.total
    if size % 128:
        split = jnp.take(x.reshape(length, plan.total, size), index, axis=1)
        split = split.reshape(length, columns)
        return split[:, : columns // 2], split[:, columns // 2 :]

    def kernel(order, source, first, second):
        for place in range(plan.total):
            out = (first, second)[place // plan.blocks]
            start = pl.multiple_of(order[place] * size, size)
            out[:, pl.ds((place % plan.blocks) * size, size)] = source[:, pl.ds(start, size)]

    whole = pl.BlockSpec(memory_space=pltpu.VMEM)
    return pl.pallas_call(
        kernel,
        out_shape=[jax.ShapeDtypeStruct((length, columns // 2), x.dtype)] * 2,
        in_specs=[pl.BlockSpec(memory_space=pltpu.SMEM), whole],
        out_specs=[whole] * 2,
        compiler_params=pltpu.CompilerParams(vmem_limit_bytes=16 * 1024 * 1024),
        cost_estimate=pl.CostEstimate(
            flops=0, transcendentals=0, bytes_accessed=4 * x.size
        ),
        name="pick_columns",
    )(index, x)


def dot(left, right):
    return jnp.dot(left, right, preferred_element_type=F32)


def dot_back(left, right):
    return lax.dot_general(left, right, (((1,), (1,)), ((), ())), preferred_element_type=F32)


def dot_over_frames(left, right):
    return lax.dot_general(left, right, (((0,), (0,)), ((), ())), preferred_element_type=F32)


def head_lanes(size, head):
    lane = lax.broadcasted_iota(jnp.int32, (1, size), 1)
    return (lane >= head * HEAD_DIM) & (lane < (head + 1) * HEAD_DIM)


def attend_kernel(q_ref, k_ref, v_ref, idq_ref, idk_ref, o_ref, total_ref):
    size = q_ref.shape[-1]
    query, keys, values = q_ref[0] * HEAD_DIM**-0.5, k_ref[0], v_ref[0]
    same = idq_ref[0] == idk_ref[0]
    mixed = jnp.zeros(query.shape, F32)
    totals = []
    for head in range(size // HEAD_DIM):
        lanes = head_lanes(size, head)
        scores = lax.dot_general(
            jnp.where(lanes, query, 0), keys, (((1,), (1,)), ((), ())), preferred_element_type=F32
        )
        scores = jnp.where(same, scores, -1e30)
        most = jnp.max(scores, axis=-1, keepdims=True)
        unnormed = jnp.exp(scores - most)
        total = jnp.sum(unnormed, axis=-1, keepdims=True)
        probs = (unnormed * (1.0 / total)).astype(BF16)
        mixed += jnp.dot(probs, jnp.where(lanes, values, 0), preferred_element_type=F32)
        totals.append(most + jnp.log(total))
    o_ref[0] = mixed.astype(BF16)
    total_ref[0] = jnp.concatenate(totals, axis=1)


def attend_back_kernel(
    q_ref, k_ref, v_ref, do_ref, total_ref, idq_ref, idk_ref, cq_ref, sq_ref, ck_ref, sk_ref,
    turn_ref, dq_ref, dk_ref, dv_ref, dk_sum, dv_sum,
):
    step = pl.program_id(1)
    size = q_ref.shape[-1]
    scale = HEAD_DIM**-0.5
    query, keys, values, grads = q_ref[0] * scale, k_ref[0], v_ref[0], do_ref[0]
    different = idk_ref[0] != idq_ref[0]

    @pl.when(step == 0)
    def _():
        dk_sum[...] = jnp.zeros_like(dk_sum)
        dv_sum[...] = jnp.zeros_like(dv_sum)

    turned_sum = jnp.zeros((size, query.shape[0]), F32)
    for head in range(size // HEAD_DIM):
        lanes = head_lanes(size, head)
        one_query = jnp.where(lanes, query, 0)
        one_grad = jnp.where(lanes, grads, 0)
        scores = lax.dot_general(
            keys, one_query, (((1,), (1,)), ((), ())), preferred_element_type=F32
        )
        probs = jnp.exp(jnp.where(different, -1e30, scores - total_ref[0, head : head + 1]))
        prob_grads = lax.dot_general(
            values, one_grad, (((1,), (1,)), ((), ())), preferred_element_type=F32
        )
        delta = jnp.sum(probs * prob_grads, axis=0, keepdims=True)
        score_grads = (probs * (prob_grads - delta)).astype(BF16)
        dk_sum[...] += jnp.dot(score_grads, one_query, preferred_element_type=F32)
        dv_sum[...] += jnp.dot(probs.astype(BF16), one_grad, preferred_element_type=F32)
        turned_sum += dot_over_frames(jnp.where(lanes, keys, 0), score_grads)

    def turned(grad, cosine, sine):
        partner = jnp.dot(grad, turn_ref[...], precision=HIGHEST, preferred_element_type=F32)
        return (grad * cosine + partner * sine).astype(BF16)

    dq_ref[0] = turned(turned_sum.T * scale, cq_ref[0], sq_ref[0])

    @pl.when(step == pl.num_programs(1) - 1)
    def _():
        dk_ref[0] = turned(dk_sum[...], ck_ref[0], sk_ref[0])
        dv_ref[0] = dv_sum[...].astype(BF16)


def attend(query, keys, values, ids, tokens=()):
    rows, length, size = query.shape
    tile = 256
    heads = size // HEAD_DIM
    whole = pl.BlockSpec((1, length, size), lambda r, t: (r, 0, 0))
    part = pl.BlockSpec((1, tile, size), lambda r, t: (r, t, 0))
    return pl.pallas_call(
        lambda *refs: attend_kernel(*refs[:5], *refs[5 + len(tokens) :]),
        out_shape=[
            jax.ShapeDtypeStruct(query.shape, BF16),
            jax.ShapeDtypeStruct((rows, length, heads), F32),
        ],
        grid=(rows, length // tile),
        in_specs=[
            part,
            whole,
            whole,
            pl.BlockSpec((1, tile, 1), lambda r, t: (r, t, 0)),
            pl.BlockSpec((1, 1, length), lambda r, t: (r, 0, 0)),
            *held(tokens),
        ],
        out_specs=[part, pl.BlockSpec((1, tile, heads), lambda r, t: (r, t, 0))],
        compiler_params=pltpu.CompilerParams(vmem_limit_bytes=VMEM_LIMIT),
        name="attend",
    )(query, keys, values, ids[:, :, None], ids[:, None, :], *tokens)


def attend_back(query, keys, values, grads, totals, ids, cosine, sine, tokens=()):
    rows, length, size = query.shape
    tile = 1024 if length <= 1024 else 256
    heads = size // HEAD_DIM
    whole = pl.BlockSpec((1, length, size), lambda r, t: (r, 0, 0))
    part = pl.BlockSpec((1, tile, size), lambda r, t: (r, t, 0))
    lane = np.arange(size)
    turn = jnp.asarray((lane[:, None] == (lane ^ (HEAD_DIM // 2))[None, :]).astype(np.float32))
    return pl.pallas_call(
        lambda *refs: attend_back_kernel(*refs[:12], *refs[12 + len(tokens) :]),
        out_shape=[jax.ShapeDtypeStruct(query.shape, BF16)] * 3,
        grid=(rows, length // tile),
        in_specs=[
            part,
            whole,
            whole,
            part,
            pl.BlockSpec((1, heads, tile), lambda r, t: (r, 0, t)),
            pl.BlockSpec((1, 1, tile), lambda r, t: (r, 0, t)),
            pl.BlockSpec((1, length, 1), lambda r, t: (r, 0, 0)),
            part,
            part,
            whole,
            whole,
            pl.BlockSpec((size, size), lambda r, t: (0, 0)),
            *held(tokens),
        ],
        out_specs=[part, whole, whole],
        scratch_shapes=[pltpu.VMEM((length, size), F32)] * 2,
        compiler_params=pltpu.CompilerParams(vmem_limit_bytes=VMEM_LIMIT),
        name="attend_back",
    )(
        query, keys, values, grads, totals.transpose(0, 2, 1), ids[:, None, :],
        ids[:, :, None], cosine, sine, cosine, sine, turn, *tokens,
    )


def set_masks(ids_ref, ids, masks, count):
    ids[...] = jnp.broadcast_to(ids_ref[0], ids.shape)
    here = ids[pl.ds(masks.shape[0] // 2, count)]
    for tap in range(masks.shape[0]):
        masks[tap] = jnp.where(ids[pl.ds(tap, count)] == here, 1.0, 0.0)


def conv_kernel(ext_ref, ids_ref, taps_ref, out_ref, frames, ids, masks):
    count, taps = out_ref.shape[1], taps_ref.shape[0]

    @pl.when(pl.program_id(1) == 0)
    def _():
        set_masks(ids_ref, ids, masks, count)

    frames[...] = ext_ref[0].astype(F32)
    total = jnp.zeros((count, frames.shape[1]), F32)
    for odd in range(8):
        shifted = frames[pl.ds(odd, frames.shape[0] - 8)]
        for tap in range(odd, taps, 8):
            part = shifted[tap - odd : tap - odd + count]
            total += part * masks[tap] * taps_ref[tap : tap + 1]
    out_ref[0] = total


def conv_back_kernel(
    ext_ref, ids_ref, grad_ref, taps_ref, dtaps_ref, dext_ref, frames, ids, masks, total, some
):
    count, taps = grad_ref.shape[1], taps_ref.shape[0]

    @pl.when(pl.program_id(1) == 0)
    def _():
        set_masks(ids_ref, ids, masks, count)

    frames[...] = ext_ref[0].astype(F32)
    grad = grad_ref[0]
    total[...] = jnp.zeros_like(total)
    rows = [None] * taps
    for odd in range(8):
        shifted = frames[pl.ds(odd, frames.shape[0] - 8)]
        some[...] = jnp.zeros_like(some)
        for tap in range(odd, taps, 8):
            kept = grad * masks[tap]
            rows[tap] = jnp.sum(shifted[tap - odd : tap - odd + count] * kept, axis=0, keepdims=True)
            some[pl.ds(tap - odd, count)] += kept * taps_ref[tap : tap + 1]
        total[pl.ds(odd, some.shape[0])] += some[...]
    dext_ref[0] = total[...]
    dtaps_ref[0] = jnp.concatenate(rows, axis=0)


def depthwise(extended, ids, taps, tokens=()):
    rows, padded, width = extended.shape
    count = padded - 32
    block = 128
    return pl.pallas_call(
        lambda *refs: conv_kernel(*refs[:3], *refs[3 + len(tokens) :]),
        out_shape=jax.ShapeDtypeStruct((rows, count, width), F32),
        grid=(rows, width // block),
        in_specs=[
            pl.BlockSpec((1, padded, block), lambda r, c: (r, 0, c)),
            pl.BlockSpec((1, padded, 1), lambda r, c: (r, 0, 0)),
            pl.BlockSpec((taps.shape[0], block), lambda r, c: (0, c)),
            *held(tokens),
        ],
        out_specs=pl.BlockSpec((1, count, block), lambda r, c: (r, 0, c)),
        scratch_shapes=[pltpu.VMEM((padded, block), F32)] * 2
        + [pltpu.VMEM((taps.shape[0], count, block), F32)],
        compiler_params=pltpu.CompilerParams(vmem_limit_bytes=16 * 1024 * 1024),
        name="depthwise",
    )(extended, ids, taps, *tokens)


def depthwise_back(extended, ids, grad, taps, tokens=()):
    rows, padded, width = extended.shape
    count = padded - 32
    block = 128
    return pl.pallas_call(
        lambda *refs: conv_back_kernel(*refs[:4], *refs[4 + len(tokens) :]),
        out_shape=[
            jax.ShapeDtypeStruct((rows, taps.shape[0], width), F32),
            jax.ShapeDtypeStruct((rows, padded, width), F32),
        ],
        grid=(rows, width // block),
        in_specs=[
            pl.BlockSpec((1, padded, block), lambda r, c: (r, 0, c)),
            pl.BlockSpec((1, padded, 1), lambda r, c: (r, 0, 0)),
            pl.BlockSpec((1, count, block), lambda r, c: (r, 0, c)),
            pl.BlockSpec((taps.shape[0], block), lambda r, c: (0, c)),
            *held(tokens),
        ],
        out_specs=[
            pl.BlockSpec((1, taps.shape[0], block), lambda r, c: (r, 0, c)),
            pl.BlockSpec((1, padded, block), lambda r, c: (r, 0, c)),
        ],
        scratch_shapes=[pltpu.VMEM((padded, block), F32)] * 2
        + [
            pltpu.VMEM((taps.shape[0], count, block), F32),
            pltpu.VMEM((padded, block), F32),
            pltpu.VMEM((padded - 8, block), F32),
        ],
        compiler_params=pltpu.CompilerParams(vmem_limit_bytes=16 * 1024 * 1024),
        name="depthwise_back",
    )(extended, ids, grad, taps, *tokens)


def segment_info(lengths, frame_total):
    segment_end = jnp.cumsum(lengths, axis=-1, dtype=jnp.int32)
    frame_index = jnp.arange(frame_total, dtype=jnp.int32)
    passed = (frame_index[None, None, :] >= segment_end[:, :, None]).astype(jnp.int32)
    segment_ids = jnp.sum(passed, axis=1, dtype=jnp.int32)
    seg_starts = jnp.sum(passed * lengths[:, :, None], axis=1, dtype=jnp.int32)
    return (segment_ids, frame_index[None, :] - seg_starts)


def layer_norm(values, gain_row):
    centred = values - jnp.mean(values, axis=-1, keepdims=True)
    inv_scale = lax.rsqrt(jnp.mean(centred * centred, axis=-1, keepdims=True) + EPSILON)
    normed = centred * inv_scale
    return (normed * gain_row, normed, inv_scale)


def norm_backward(gradient, gain_row, normed, inv_scale):
    scaled = gradient * gain_row
    gain_grad = jnp.sum(gradient * normed, axis=0)
    centred_mean = jnp.mean(scaled, axis=-1, keepdims=True)
    product_mean = jnp.mean(scaled * normed, axis=-1, keepdims=True)
    return (inv_scale * (scaled - centred_mean - normed * product_mean), gain_grad)


def swish_slope(values):
    gate_sig = jax.nn.sigmoid(values)
    return gate_sig * (1.0 + values * (1.0 - gate_sig))


def neighbours(x, width, axis):
    size, length = lax.axis_size("wide"), x.shape[axis]
    up = [(i, i + 1) for i in range(size - 1)]
    before = lax.ppermute(lax.slice_in_dim(x, length - width, length, axis=axis), "wide", up)
    after = lax.ppermute(
        lax.slice_in_dim(x, 0, width, axis=axis), "wide", [(j, i) for i, j in up]
    )
    return before, after


def half_turn(values):
    half = HEAD_DIM // 2
    lane = lax.broadcasted_iota(jnp.int32, (1, values.shape[-1]), 1) % HEAD_DIM
    ahead = jnp.roll(values, -half, axis=-1)
    behind = jnp.roll(values, half, axis=-1)
    return jnp.where(lane < half, -ahead, behind)


def per_device(
    inputs,
    lengths,
    ffn1_in,
    ffn1_out,
    attn_qkv,
    attn_out,
    conv_in,
    depth_kernel,
    conv_out,
    ffn2_in,
    ffn2_out,
    norm_gains,
    cotangent,
):
    wide, rows = lax.axis_size("wide"), lax.axis_size("rows")
    plan = Plan(wide, rows)
    row_count, frames_here, width = inputs.shape
    tokens = row_count * frames_here
    frame_total = frames_here * wide
    taps = depth_kernel.shape[0]
    half_width = taps // 2
    me = lax.axis_index("wide")
    orders = plan.orders()
    segment_ids, position = segment_info(lengths, frame_total)

    def packed_shards(shards):
        parts = []
        for shard in shards:
            for column in range(0, shard.shape[1], width):
                parts.append(shard[:, column : column + width])
        return jnp.concatenate(parts, axis=0) if len(parts) > 1 else parts[0]

    def weights_lane(*shards):
        shapes = [shard.shape for shard in shards]
        return Lane(
            gather_lane(
                plan, packed_shards(shards), lambda held: assemble(plan, held, shapes, orders)
            )
        )

    def small_lane(small):
        flip = 1
        while flip < plan.total:
            small = jnp.concatenate([small, (yield small, plan.flip_pairs(flip))], axis=1)
            flip *= 2
        return dot_back(small, small_pick.astype(BF16))

    feature = jnp.arange(width, dtype=jnp.int32)
    block = width // plan.total
    small_source = (feature // block ^ lax.axis_index(BOTH)) * block + feature % block
    small_pick = feature[:, None] == small_source[None, :]
    small = Lane(small_lane(jnp.concatenate([norm_gains, depth_kernel], axis=0)))
    g1, g2 = weights_lane(ffn1_in), weights_lane(ffn1_out)
    w_qkv = lax.all_gather(attn_qkv, BOTH, axis=0, tiled=True)
    wides = (attn_out, conv_in, conv_out)
    middle = lax.all_gather(jnp.concatenate(wides, axis=1), BOTH, axis=0, tiled=True)
    cuts = np.cumsum([0] + [shard.shape[1] for shard in wides])
    w_attn_out, w_conv_in, w_conv_out = (
        middle[:, start:stop] for start, stop in zip(cuts[:-1], cuts[1:])
    )
    w_ffn2_in = lax.all_gather(ffn2_in, BOTH, axis=0, tiled=True)
    g4 = weights_lane(ffn2_out)

    source = jnp.repeat(jnp.concatenate(orders), block) * block + feature % block
    tree_pick = (feature[:, None] == source[None, :]).astype(BF16)
    group = width // wide
    head_source = (feature // group ^ me) * group + feature % group
    head_pick = (feature[:, None] == head_source[None, :]).astype(BF16)

    def pick(x):
        both = dot(x, tree_pick).astype(BF16)
        return both[:, : width // 2], both[:, width // 2 :]

    def to_groups(x):
        return dot(x, head_pick).astype(BF16).reshape(tokens, wide, group).transpose(1, 0, 2)

    def from_groups(x):
        return dot_back(x.transpose(1, 0, 2).reshape(tokens, width), head_pick).astype(BF16)

    offset = me * frames_here
    padded_ids = jnp.pad(segment_ids, ((0, 0), (half_width, 32 - half_width)), constant_values=-1)
    edge_ids = lax.dynamic_slice_in_dim(padded_ids, offset, frames_here + 32, 1)
    edge_ids = edge_ids.astype(F32)[:, :, None]
    local_position = lax.dynamic_slice_in_dim(position, offset, frames_here, 1)
    by_device = jnp.arange(wide, dtype=jnp.int32) ^ me

    def row_order(x):
        x = x.reshape(row_count, wide, frames_here)
        return jnp.take(x, by_device, axis=1).reshape(row_count, frame_total)

    row_ids, row_position = row_order(segment_ids), row_order(position)

    def rotation(at, size):
        lane = jnp.arange(size, dtype=jnp.int32) % HEAD_DIM
        frequency = jnp.power(
            10000.0, -2.0 * (lane % (HEAD_DIM // 2)).astype(F32) / HEAD_DIM
        )
        angles = at.astype(F32)[..., None] * frequency
        sign = jnp.where(lane < HEAD_DIM // 2, 1.0, -1.0)
        return jnp.cos(angles), jnp.sin(angles), sign

    cosine, sine, _ = rotation(local_position.reshape(tokens), HEAD_DIM)
    cosine = jnp.tile(cosine, (1, HEADS))
    sine = jnp.tile(sine, (1, HEADS))
    row_cosine, row_sine, sign = rotation(row_position, group)
    row_sine = row_sine * sign

    tables = (row_cosine, row_sine, cosine, sine, edge_ids)
    def follow(lane, leader):
        lane.operand = after(lane.operand, jax.tree.leaves(ready(leader)))
        lane.go()

    step(go=[g1, small])
    for _ in range(3):
        step(land=[small], go=[small])
    step(land=[g1, small], go=[small])
    follow(g1, small)
    finish(small)
    gains, kernel = small.result[: norm_gains.shape[0]], small.result[norm_gains.shape[0] :]
    residual = inputs.astype(F32).reshape(tokens, width)
    ffn1_norm, ffn1_normed, ffn1_scale = layer_norm(residual, gains[0])
    ffn1_hidden = after(ffn1_norm.astype(BF16), tables)
    follow(g2, g1)
    step(land=[g1])
    g1.operand = after(g1.operand, [gains])
    g1.go()
    step(land=[g2])
    follow(g2, g1)
    for _ in range(2):
        step(land=[g1], go=[g1])
        step(land=[g2])
        follow(g2, g1)
    follow(g4, g2)
    (w_ffn1_in,) = finish(g1)
    before_1 = dot(ffn1_hidden, w_ffn1_in)
    after_1 = (before_1 * jax.nn.sigmoid(before_1)).astype(BF16)
    (w_ffn1_out,) = finish(g2)
    first = residual + 0.5 * dot(after_1, w_ffn1_out)
    attn_norm, attn_normed, attn_scale = layer_norm(first, gains[1])
    attn_hidden = attn_norm.astype(BF16)
    packed = dot(attn_hidden, w_qkv)
    step(land=[g4], go=[g4], since=[packed])
    queries = packed[:, :width]
    keys = packed[:, width : 2 * width]
    queries = (queries * cosine + half_turn(queries) * sine).astype(BF16)
    keys = (keys * cosine + half_turn(keys) * sine).astype(BF16)
    values = packed[:, 2 * width :].astype(BF16)
    heads = Lane(
        heads_lane(
            plan,
            jnp.concatenate([to_groups(queries), to_groups(keys), to_groups(values)], axis=-1),
        )
    )

    def as_rows(x):
        x = x.reshape(wide, row_count, frames_here, group)
        return x.transpose(1, 0, 2, 3).reshape(row_count, frame_total, group)

    def as_blocks(x):
        x = x.reshape(row_count, wide, frames_here, group)
        return x.transpose(1, 0, 2, 3).reshape(wide, tokens, group)

    step(go=[heads])
    step(land=[heads], go=[heads])
    step(land=[g4], since=ready(heads)[0])
    arrived = finish(heads)
    hold(g4, arrived)
    row_queries = as_rows(arrived[..., :group])
    row_keys = as_rows(arrived[..., group : 2 * group])
    row_values = as_rows(arrived[..., 2 * group :])
    mixed_rows, row_totals = attend(row_queries, row_keys, row_values, row_ids)
    heads = Lane(heads_lane(plan, as_blocks(mixed_rows)))
    step(go=[heads])
    step(land=[heads], go=[heads])
    step(land=[g4], go=[g4], since=ready(heads)[0])
    mixed = from_groups(finish(heads))
    second = first + dot(mixed, w_attn_out)
    conv_norm, conv_normed, conv_scale = layer_norm(second, gains[2])
    conv_hidden = conv_norm.astype(BF16)
    gated = dot(conv_hidden, w_conv_in)
    gate_sig = jax.nn.sigmoid(gated[:, width:])
    glu = (gated[:, :width] * gate_sig).astype(BF16).reshape(row_count, frames_here, width)
    before, after_frames = neighbours(glu, half_width, 1)
    extended = jnp.concatenate(
        [before, glu, after_frames, jnp.zeros((row_count, 32 - 2 * half_width, width), BF16)],
        axis=1,
    )
    step(land=[g4], go=[g4], since=[gate_sig])
    convolved = depthwise(extended, edge_ids, kernel).reshape(tokens, width)
    inner_out, inner_normed, inner_scale = layer_norm(convolved, gains[3])
    activated = (inner_out * jax.nn.sigmoid(inner_out)).astype(BF16)
    third = second + dot(activated, w_conv_out)
    ffn2_norm, ffn2_normed, ffn2_scale = layer_norm(third, gains[4])
    ffn2_hidden = ffn2_norm.astype(BF16)
    before_2 = dot(ffn2_hidden, w_ffn2_in)
    after_2 = (before_2 * jax.nn.sigmoid(before_2)).astype(BF16)
    (w_ffn2_out,) = finish(g4)
    fourth = third + 0.5 * dot(after_2, w_ffn2_out)
    final_out, final_normed, final_scale = layer_norm(fourth, gains[5])
    layer_out = final_out.astype(BF16).reshape(inputs.shape)

    def grads(*pairs, split=0):
        lefts, rights = [left for left, _ in pairs], [right for _, right in pairs]
        return Lane(grad_lane(plan, lefts, rights, split))

    gradient, gain_final = norm_backward(
        cotangent.astype(F32).reshape(tokens, width), gains[5], final_normed, final_scale
    )
    branch = (0.5 * gradient).astype(BF16)
    r1 = grads((pick_columns(plan, after_2, orders), branch))
    r1.go()
    before_grad = (dot_back(branch, w_ffn2_out) * swish_slope(before_2)).astype(BF16)
    r2 = grads((pick(ffn2_hidden), before_grad))
    r2.go()
    step(land=[r1], go=[r1])
    input_grad, gain_ffn2 = norm_backward(
        dot_back(before_grad, w_ffn2_in), gains[4], ffn2_normed, ffn2_scale
    )
    gradient = gradient + input_grad
    conv_branch = after(gradient.astype(BF16), jax.tree.leaves(ready(r1)))
    act_grad = dot_back(conv_branch, w_conv_out) * swish_slope(inner_out)
    conv_grad, gain_inner = norm_backward(act_grad, gains[3], inner_normed, inner_scale)
    step(land=[r2], go=[r2])
    kernel_terms, ext_grad = depthwise_back(
        extended,
        edge_ids,
        conv_grad.reshape(row_count, frames_here, width),
        kernel,
        jax.tree.leaves(ready(r1, r2)),
    )
    grad_kernel = jnp.sum(kernel_terms, axis=0)
    end = half_width + frames_here
    rims = ext_grad[:, :half_width], ext_grad[:, end : end + half_width]
    to_before, to_after = (rim.astype(BF16) for rim in rims)
    up = [(i, i + 1) for i in range(wide - 1)]
    from_before = lax.ppermute(to_after, "wide", up).astype(F32)
    from_after = lax.ppermute(to_before, "wide", [(j, i) for i, j in up]).astype(F32)
    middle = jnp.zeros((row_count, frames_here - 2 * half_width, width), F32)
    glu_grad = ext_grad[:, half_width:end] + jnp.concatenate(
        [from_before, middle, from_after], axis=1
    )
    glu_grad = glu_grad.reshape(tokens, width)
    gated_grad = jnp.concatenate(
        [glu_grad * gate_sig, glu_grad * gated[:, :width] * gate_sig * (1.0 - gate_sig)],
        axis=-1,
    ).astype(BF16)
    norm_grad, gain_conv = norm_backward(
        dot_back(gated_grad, w_conv_in), gains[2], conv_normed, conv_scale
    )
    gradient = gradient + norm_grad
    attn_branch = gradient.astype(BF16)
    head_grads = dot_back(attn_branch, w_attn_out).astype(BF16)
    heads = Lane(heads_lane(plan, to_groups(head_grads)))
    r3 = grads(
        (pick(activated), conv_branch), (pick(conv_hidden), gated_grad), (pick(mixed), attn_branch)
    )
    step(go=[heads, r3])
    step(land=[heads], go=[heads])
    step(land=[r1, r3], go=[r1, r3], since=ready(heads)[0])
    row_grads = as_rows(finish(heads))
    query_grad, key_grad, value_grad = attend_back(
        row_queries,
        row_keys,
        row_values,
        row_grads,
        row_totals,
        row_ids,
        row_cosine,
        row_sine,
        jax.tree.leaves(ready(r1, r3)),
    )
    heads = Lane(
        heads_lane(
            plan,
            jnp.concatenate(
                [as_blocks(query_grad), as_blocks(key_grad), as_blocks(value_grad)], axis=-1
            ),
        )
    )
    step(go=[heads])
    step(land=[heads], go=[heads])
    step(land=[r1, r2, r3], go=[r2, r3], since=ready(heads)[0])
    returned = finish(heads)
    returned = after(returned, jax.tree.leaves(ready(r1, r2, r3)))
    hold(r1, returned)
    packed_grad = jnp.concatenate(
        [from_groups(returned[..., part * group : (part + 1) * group]) for part in range(3)],
        axis=-1,
    )
    packed_grad = lax.optimization_barrier(packed_grad)
    r6 = grads((pick(attn_hidden), packed_grad), split=0)
    r6.go()
    norm_grad, gain_attn = norm_backward(
        dot_back(packed_grad, w_qkv), gains[1], attn_normed, attn_scale
    )
    gradient = gradient + norm_grad
    branch = (0.5 * gradient).astype(BF16)
    step(land=[r2], go=[r2], since=[packed_grad])
    branch = step(land=[r6], go=[r6], chain=branch)
    r7 = grads((pick_columns(plan, after_1, orders), branch), split=1)
    r7.go()
    before_grad = (dot_back(branch, w_ffn1_out) * swish_slope(before_1)).astype(BF16)
    before_grad = lax.optimization_barrier(before_grad)
    r8 = grads((pick(ffn1_hidden), before_grad), split=2)
    r8.go()
    step(land=[r1, r2, r3], go=[r1, r2, r3], since=[branch])
    step(land=[r7, r8], go=[r7, r8])
    before_grad = after(before_grad, jax.tree.leaves(ready(r1, r2, r3, r7, r8)))
    input_grad, gain_ffn1 = norm_backward(
        dot_back(before_grad, w_ffn1_in), gains[0], ffn1_normed, ffn1_scale
    )
    gradient = gradient + input_grad
    grad_gains = jnp.stack([gain_ffn1, gain_attn, gain_conv, gain_inner, gain_ffn2, gain_final])
    small_sums = jnp.concatenate([grad_gains, grad_kernel], axis=0)
    small_sums = jnp.dot(small_sums, tree_pick.astype(F32), precision=HIGHEST)
    r9 = Lane(small_grad_lane(plan, small_sums))
    finish(r1, r2, since=[before_grad])
    step(land=[r3], go=[r3], since=[before_grad])
    hold(r9, *r1.result, *r2.result)
    step(land=[r6], go=[r6])
    step(land=[r7], go=[r7], since=[input_grad, *waited(r6)])
    while r8.operand is not None:
        step(land=[r9], since=jax.tree.leaves(ready(r8)))
        r9.go()
        step(land=[r7, r8], go=[r7, r8])
        step(land=[r1, r2, r3, r6], go=[r1, r2, r3, r6], since=jax.tree.leaves(ready(r8))[:1])
    finish(r1, r2, r3, r6, r7, r9)
    (grad_ffn1_in,), (grad_ffn1_out,), (grad_qkv,) = r8.result, r7.result, r6.result
    grad_conv_out, grad_conv_in, grad_attn_out = r3.result
    (grad_ffn2_in,), (grad_ffn2_out,), small_shard = r2.result, r1.result, r9.result
    shard_gains, shard_kernel = small_shard[: grad_gains.shape[0]], small_shard[grad_gains.shape[0] :]

    return (
        layer_out,
        gradient.astype(BF16).reshape(inputs.shape),
        grad_ffn1_in,
        grad_ffn1_out,
        grad_qkv,
        grad_attn_out,
        grad_conv_in,
        shard_kernel,
        grad_conv_out,
        grad_ffn2_in,
        grad_ffn2_out,
        shard_gains,
    )


def solution(mesh):
    frames = P("rows", "wide", None)
    split_rows = P(BOTH, None)
    split_columns = P(None, BOTH)
    weights = (split_rows,) * 5 + (split_columns,) + (split_rows,) * 3 + (split_columns,)
    return jax.shard_map(
        per_device,
        mesh=mesh,
        in_specs=(frames, P("rows", None)) + weights + (frames,),
        out_specs=(frames, frames) + weights,
        check_vma=False,
    )
```
